512 devices in a mesh: mp: 16 (over z), trow: 4 (over x), tcol: 8 (over y, core).
Axes of the slice: x: 4, y: 4, z: 16, core: 2. Of those that a mesh axis runs over, the one named last changes fastest.
Arguments:
- gram: float32 [16, 4096, 4096], P('mp', 'trow', 'tcol'), as said below
- rhs: float32 [256, 4096], P(('mp', 'tcol'), 'trow'), may hold values from -6 to 6
- guess: float32 [256, 4096], P(('mp', 'tcol'), 'trow'), may hold values from -6 to 6
Outputs:
- merged: float32 [256, 4096], P(('mp', 'tcol'), 'trow')
- residual: float32 [256, 4096], P(('mp', 'tcol'), 'trow')
The draws below stay inside these ranges and needn't reach their ends.
Inputs may be any that keep to these rules, and one draw needn't show every extreme that they name: gram holds 16 symmetric positive definite matrices, one per model.
All inputs are finite; a program needn't handle non-finite values.
Results may differ from the reference program's by a relative error of at most 0.0003.
Values sent between devices are 32-bit elements; how exact they have to be, the bound alone decides.
No kernel may reach another device: no remote copies, remote signals or barrier semaphores. Data moves between devices by JAX's collectives and lax.ppermute only.
A program may use at most 64 MiB of HBM per device.

```python
import math
import jax
import jax.numpy as jnp
from jax import lax

D = 4096
COLS = 256
ITERS = 2
MODELS = 16


def draw_gram(key, part):
    first, second, third, fourth = jax.random.split(key, 4)
    position = jnp.arange(D, dtype=jnp.float32)
    trend = 1.0 + 2.0 * position / (D - 1)
    lower = -1.0
    lowest = math.log(0.32)
    own_entries = jax.random.uniform(first, (MODELS, D, D), jnp.float32, lower, 1.0)
    shared_entries = jax.random.uniform(fourth, (D, D), jnp.float32, lower, 1.0)
    raw_entries = 0.6 * shared_entries[None, :, :] + 0.8 * own_entries
    symmetric = 0.5 * (raw_entries + jnp.swapaxes(raw_entries, 1, 2))
    common = jnp.exp(jax.random.uniform(second, (D,), jnp.float32, lowest, 0.0)) * trend
    factor = jnp.exp(jax.random.uniform(third, (MODELS, D), jnp.float32, math.log(0.5), math.log(2.0)))
    scaling = jnp.sqrt(common[None, :] * factor / MODELS)
    diagonal_mask = jnp.arange(D)[:, None] == jnp.arange(D)[None, :]
    inner = jnp.where(diagonal_mask[None, :, :], 1.0, 0.8 / math.sqrt(D) * symmetric)
    return scaling[:, :, None] * scaling[:, None, :] * inner


def block_levels(rng, extent, pieces, least, top_value):
    level = 1.0
    for dim, shards_of in pieces:
        heights = jax.random.uniform(jax.random.fold_in(jax.random.fold_in(rng, 6), dim), (shards_of,), jnp.float32, least / len(pieces), top_value / len(pieces))
        level = level * jnp.repeat(jnp.exp(heights), extent[dim] // shards_of).reshape((-1,) + (1,) * (len(extent) - 1 - dim))
    return level


def centred(rng, shape, scale, reach, pieces=(), held_as=jnp.bfloat16):
    array = jax.random.normal(rng, shape, jnp.float32) * scale
    if len(pieces) > 0:
        array = block_levels(rng, shape, pieces, -0.22, 0.18) * array
    return jnp.clip(array, min=-reach, max=reach).astype(held_as)


def setup_inputs(seed: int = 0) -> dict:
    key_list = jax.random.split(jax.random.key(seed), 4)
    gram = draw_gram(jax.random.fold_in(key_list[3], 71), 0)
    rhs = centred(key_list[1], (COLS, D), 1.0, 6.0, ((0, 128), (1, 4)), jnp.float32)
    guess = centred(key_list[2], (COLS, D), 1.0, 6.0, ((0, 128), (1, 4)), jnp.float32)
    return {"gram": gram, "rhs": rhs, "guess": guess}


def reference(gram, rhs, guess):
    total = jnp.sum(gram, axis=0)

    def apply_total(vector):
        return lax.dot_general(vector, total, (((1,), (1,)), ((), ())), precision=lax.Precision.HIGHEST, preferred_element_type=jnp.float32)

    merged = guess
    residual = rhs - apply_total(guess)
    direction = residual
    norm_now = jnp.sum(residual * residual, axis=1)
    for step in range(ITERS):
        image = apply_total(direction)
        alpha = norm_now / jnp.sum(direction * image, axis=1)
        merged = merged + alpha[:, None] * direction
        residual = residual - alpha[:, None] * image
        norm_next = jnp.sum(residual * residual, axis=1)
        direction = residual + (norm_next / norm_now)[:, None] * direction
        norm_now = norm_next
    return merged, residual
```

```python
import jax
import jax.numpy as jnp
from jax import lax
from jax.sharding import Mesh, PartitionSpec as P

MP = ("zh", "zl")
PLANE = ("trow", "tcol")
HIGHEST = lax.Precision.HIGHEST


def dot(lhs, rhs, lhs_dim, rhs_dim):
    return lax.dot_general(
        lhs,
        rhs,
        (((lhs_dim,), (rhs_dim,)), ((), ())),
        precision=HIGHEST,
        preferred_element_type=jnp.float32,
    )


def exchange(pieces, axes):
    return lax.all_to_all(pieces, axes, 0, 0, tiled=True)


def spread(block, axes, count):
    return exchange(jnp.broadcast_to(block[None], (count,) + block.shape), axes)


def transposed(vector, sizes):
    trow, tcol = sizes["trow"], sizes["tcol"]
    own, wide = vector.shape
    half = wide // 2
    core = lax.axis_index("tcol") % 2
    halves = (vector[:, :half], vector[:, half:])
    got = []
    for turn in range(2):
        pairs = []
        for i in range(trow):
            for j in range(tcol):
                q, h = j // 2, j % 2
                pairs.append((i * tcol + j, q * tcol + 2 * i + (h ^ turn)))
        low = core == turn
        sent = jnp.where(low, halves[0], halves[1])
        got.append(lax.ppermute(sent, PLANE, pairs))
    first = core == 0
    return jnp.stack([jnp.where(first, got[0], got[1]), jnp.where(first, got[1], got[0])])


def shards(sizes, gram, rhs, guess):
    zh, zl, trow, tcol = sizes["zh"], sizes["zl"], sizes["trow"], sizes["tcol"]
    mp = zh * zl
    tile = gram[0]
    rows, cols = tile.shape
    own = rhs.shape[0]
    thin = cols // zh

    cut = tile.reshape(zl, rows // zl, zh, thin).transpose(2, 0, 1, 3).reshape(mp * (rows // zl), thin)
    part = lax.psum_scatter(cut, MP, scatter_dimension=0, tiled=True)
    total = lax.all_gather(part, "zl", axis=0, tiled=True)

    flipped = transposed(guess, sizes)
    over_mp = spread(flipped, MP, mp)
    over_mp = over_mp.transpose(1, 0, 2, 3).reshape(2 * mp * own, cols)
    block = spread(over_mp, "trow", trow).reshape(trow * 2 * mp * own, cols)
    terms = dot(block, tile, 1, 1)
    terms = exchange(terms.reshape(tcol, mp * own, rows), "tcol").sum(0)
    terms = exchange(terms.reshape(mp, own, rows), MP).sum(0)
    first = rhs - terms

    near = spread(first, "zh", zh).reshape(zh * own, rows)
    wide = spread(near, "tcol", tcol).reshape(tcol * zh * own, rows)
    second = spread(dot(wide, total, 1, 0), "trow", trow).sum(0)
    terms = dot(second, total, 1, 1)
    pieces = jnp.concatenate([terms, second], axis=1).reshape(tcol, zh * own, rows + thin)
    pieces = exchange(pieces, "tcol")
    terms = pieces[:, :, :rows].sum(0)
    mine = lax.dynamic_slice(
        pieces, (2 * lax.axis_index("trow"), 0, rows), (2, zh * own, thin)
    )
    pieces = jnp.concatenate([terms, mine[0], mine[1]], axis=1).reshape(zh, own, rows + 2 * thin)
    pieces = exchange(pieces, "zh")
    third = pieces[:, :, :rows].sum(0)
    second = pieces[:, :, rows:].reshape(zh, own, 2, thin).transpose(1, 2, 0, 3).reshape(own, rows)

    def norm(v):
        return jnp.sqrt(jnp.sum(v * v, axis=1))

    def inverse(x):
        return jnp.where(x > 0, 1.0 / jnp.where(x > 0, x, 1.0), 0.0)

    f0 = norm(first)
    e0 = first * inverse(f0)[:, None]
    s0 = jnp.sum(e0 * second, axis=1)
    rest = second - s0[:, None] * e0
    s1 = norm(rest)
    e1 = rest * inverse(s1)[:, None]
    t0 = jnp.sum(e0 * third, axis=1)
    t1 = jnp.sum(e1 * (third - t0[:, None] * e0), axis=1)
    f0, s0, s1, t0, t1 = jnp.moveaxis(spread(jnp.stack([f0, s0, s1, t0, t1]), "trow", trow), 1, 0)

    norm_first = jnp.sum(f0 * f0, 0)
    alpha = norm_first / jnp.sum(f0 * s0, 0)
    r0, r1 = f0 - alpha * s0, -alpha * s1
    norm_next = jnp.sum(r0 * r0 + r1 * r1, 0)
    beta = norm_next / norm_first
    d0, d1 = r0 + beta * f0, r1
    i0, i1 = s0 - alpha * t0 + beta * s0, s1 - alpha * t1 + beta * s1
    alpha_next = norm_next / jnp.sum(d0 * i0 + d1 * i1, 0)

    alpha, beta, alpha_next = alpha[:, None], beta[:, None], alpha_next[:, None]
    residual = first - alpha * second
    direction = residual + beta * first
    image = second - alpha * third + beta * second
    merged = guess + alpha * first + alpha_next * direction
    return merged, residual - alpha_next * image


def solution(mesh):
    mp, trow, tcol = (mesh.shape[a] for a in ("mp", "trow", "tcol"))
    zl = 4 if mp % 4 == 0 and mp > 4 else 2
    sizes = {"zh": mp // zl, "zl": zl, "trow": trow, "tcol": tcol}
    split = Mesh(mesh.devices.reshape(tuple(sizes.values())), tuple(sizes))
    in_specs = (P(MP, "trow", "tcol"), P(MP + ("tcol",), "trow"), P(MP + ("tcol",), "trow"))
    out_specs = (P(MP + ("tcol",), "trow"), P(MP + ("tcol",), "trow"))

    def body(gram, rhs, guess):
        return shards(sizes, gram, rhs, guess)

    return jax.shard_map(body, mesh=split, in_specs=in_specs, out_specs=out_specs, check_vma=False)
```

```python
import jax
import jax.numpy as jnp
from jax import lax
from jax.sharding import Mesh, PartitionSpec as P

MP = ("zk", "zb")
PLANE = ("trow", "tcol")
SHARD = ("trow", "zb")
HIGHEST = lax.Precision.HIGHEST


def dot(lhs, rhs, lhs_dim, rhs_dim):
    return lax.dot_general(
        lhs,
        rhs,
        (((lhs_dim,), (rhs_dim,)), ((), ())),
        precision=HIGHEST,
        preferred_element_type=jnp.float32,
    )


def exchange(pieces, axes):
    return lax.all_to_all(pieces, axes, 0, 0, tiled=True)


def spread(block, axes, count):
    return exchange(jnp.broadcast_to(block[None], (count,) + block.shape), axes)


def ordered(flag, mine, other):
    return jnp.where(flag == 0, mine, other), jnp.where(flag == 0, other, mine)


def transposed(vector, sizes):
    trow, tcol = sizes["trow"], sizes["tcol"]
    half = vector.shape[1] // 2
    core = lax.axis_index("tcol") % 2
    halves = (vector[:, :half], vector[:, half:])
    got = []
    for turn in range(2):
        pairs = []
        for i in range(trow):
            for j in range(tcol):
                q, h = j // 2, j % 2
                pairs.append((i * tcol + j, q * tcol + 2 * i + (h ^ turn)))
        sent = jnp.where(core == turn, halves[0], halves[1])
        got.append(lax.ppermute(sent, PLANE, pairs))
    return jnp.stack(ordered(core, got[0], got[1]))


def shards(sizes, gram, rhs, guess):
    zk, zb, trow, tcol = sizes["zk"], sizes["zb"], sizes["trow"], sizes["tcol"]
    mp = zk * zb
    tile = gram[0]
    rows, cols = tile.shape
    own = rhs.shape[0]
    part_rows = rows // zb
    half = lax.axis_index("zb")

    cut = tile.reshape(zb, zk, part_rows // zk, cols).transpose(1, 0, 2, 3).reshape(rows, cols)
    part = lax.psum_scatter(cut, MP, scatter_dimension=0, tiled=True)
    total = lax.all_gather(part, "zk", axis=0, tiled=True)

    flipped = transposed(guess, sizes)
    over_mp = spread(flipped, MP, mp)
    over_mp = over_mp.transpose(1, 0, 2, 3).reshape(2 * mp * own, cols)
    block = spread(over_mp, "trow", trow).reshape(trow * 2 * mp * own, cols)
    terms = dot(block, tile, 1, 1)
    terms = exchange(terms.reshape(tcol, mp * own, rows), "tcol").sum(0)
    terms = exchange(terms.reshape(mp, own, rows), MP).sum(0)
    first = rhs - terms

    def halves(vector):
        low, high = vector[:, :part_rows], vector[:, part_rows:]
        return jnp.where(half == 0, low, high), jnp.where(half == 0, high, low)

    kept, given = halves(first)
    got = lax.ppermute(given, "zb", [(0, 1), (1, 0)])
    near = jnp.concatenate(ordered(half, kept, got))
    wide = spread(near, "tcol", tcol).reshape(tcol * zb * own, part_rows)
    second = spread(dot(wide, total, 1, 0), SHARD, trow * zb).sum(0)
    terms = dot(second, total, 1, 1)
    pieces = jnp.concatenate([terms, second], axis=1).reshape(tcol, zb * own, part_rows + cols)
    pieces = exchange(pieces, "tcol")
    third = pieces[:, :, :part_rows].sum(0)
    second = lax.dynamic_slice(
        pieces, (2 * lax.axis_index("trow"), 0, part_rows), (2, zb * own, cols)
    )
    second = jnp.concatenate([second[0], second[1]], axis=1)

    def inner(u, v):
        return jnp.sum(u * v, axis=1, keepdims=True)

    def inverse(x):
        return jnp.where(x > 0, 1.0 / jnp.where(x > 0, x, 1.0), 0.0)

    here, _ = halves(second)
    f0 = jnp.sqrt(inner(near, near))
    e0 = near * inverse(f0)
    s0 = inner(e0, here)
    rest = here - s0 * e0
    s1 = jnp.sqrt(inner(rest, rest))
    e1 = rest * inverse(s1)
    t0 = inner(e0, third)
    t1 = inner(e1, third - t0 * e0)
    known = jnp.concatenate([third, jnp.pad(jnp.concatenate([f0, s0, s1, t0, t1], axis=1), ((0, 0), (0, 123)))], axis=1)
    wide_known = part_rows + 128
    pieces = jnp.broadcast_to(known[None], (trow,) + known.shape).reshape(trow * zb, own, wide_known)
    pieces = exchange(pieces, SHARD)
    f0, s0, s1, t0, t1 = (pieces[:, :, part_rows + n : part_rows + n + 1] for n in range(5))
    third = lax.dynamic_slice(
        pieces, (zb * lax.axis_index("trow"), 0, 0), (zb, own, part_rows)
    )
    third = jnp.concatenate([third[0], third[1]], axis=1)
    second = jnp.where(half == 0, second[:own], second[own:])

    norm_first = jnp.sum(f0 * f0, 0)
    alpha = norm_first / jnp.sum(f0 * s0, 0)
    r0, r1 = f0 - alpha * s0, -alpha * s1
    norm_next = jnp.sum(r0 * r0 + r1 * r1, 0)
    beta = norm_next / norm_first
    d0, d1 = r0 + beta * f0, r1
    i0, i1 = s0 - alpha * t0 + beta * s0, s1 - alpha * t1 + beta * s1
    alpha_next = norm_next / jnp.sum(d0 * i0 + d1 * i1, 0)

    residual = first - alpha * second
    direction = residual + beta * first
    image = second - alpha * third + beta * second
    merged = guess + alpha * first + alpha_next * direction
    return merged, residual - alpha_next * image


def solution(mesh):
    mp, trow, tcol = (mesh.shape[a] for a in ("mp", "trow", "tcol"))
    sizes = {"zk": mp // 2, "zb": 2, "trow": trow, "tcol": tcol}
    split = Mesh(mesh.devices.reshape(tuple(sizes.values())), tuple(sizes))
    in_specs = (P(MP, "trow", "tcol"), P(MP + ("tcol",), "trow"), P(MP + ("tcol",), "trow"))
    out_specs = (P(MP + ("tcol",), "trow"), P(MP + ("tcol",), "trow"))

    def body(gram, rhs, guess):
        return shards(sizes, gram, rhs, guess)

    return jax.shard_map(body, mesh=split, in_specs=in_specs, out_specs=out_specs, check_vma=False)
```

```python
import jax
import jax.numpy as jnp
from jax import lax
from jax.experimental import pallas as pl
from jax.experimental.pallas import tpu as pltpu
from jax.sharding import Mesh, PartitionSpec as P

MP = ("zk", "zb")
TCOL = ("y", "core")
PLANE = ("trow",) + TCOL
SHARD = ("trow", "zb")
HIGHEST = lax.Precision.HIGHEST


def dot(lhs, rhs, lhs_dim, rhs_dim):
    return lax.dot_general(
        lhs,
        rhs,
        (((lhs_dim,), (rhs_dim,)), ((), ())),
        precision=HIGHEST,
        preferred_element_type=jnp.float32,
    )


def exchange(pieces, axes):
    return lax.all_to_all(pieces, axes, 0, 0, tiled=True)


def spread(block, axes, count):
    return exchange(jnp.broadcast_to(block[None], (count,) + block.shape), axes)


def ordered(flag, mine, other):
    return jnp.where(flag == 0, mine, other), jnp.where(flag == 0, other, mine)


def transposed(vector, sizes):
    trow, tcol = sizes["trow"], sizes["y"] * sizes["core"]
    half = vector.shape[1] // 2
    core = lax.axis_index("core")
    halves = (vector[:, :half], vector[:, half:])
    got = []
    for turn in range(2):
        pairs = []
        for i in range(trow):
            for j in range(tcol):
                q, h = j // 2, j % 2
                pairs.append((i * tcol + j, q * tcol + 2 * i + (h ^ turn)))
        sent = jnp.where(core == turn, halves[0], halves[1])
        got.append(lax.ppermute(sent, PLANE, pairs))
    return jnp.stack(got)


def reordered(tile, order, chunk):
    def body(source, target, done):
        copies = [
            pltpu.make_async_copy(
                source.at[pl.ds(n * chunk, chunk)],
                target.at[pl.ds(at * chunk, chunk)],
                done.at[at],
            )
            for at, n in enumerate(order)
        ]
        for copy in copies:
            copy.start()
        for copy in copies:
            copy.wait()

    return pl.pallas_call(
        body,
        out_shape=jax.ShapeDtypeStruct(tile.shape, tile.dtype),
        in_specs=[pl.BlockSpec(memory_space=pl.ANY)],
        out_specs=pl.BlockSpec(memory_space=pl.ANY),
        scratch_shapes=[pltpu.SemaphoreType.DMA((len(order),))],
        cost_estimate=pl.CostEstimate(flops=0, bytes_accessed=2 * tile.size * 4, transcendentals=0),
    )(tile)


def reduced(mp, gram, guess):
    tile = gram[0]
    rows, cols = tile.shape
    chunk = rows // mp
    order = []
    for k in range(mp // 2):
        order += [k, mp - 1 - k]
    cut = reordered(tile, order, chunk)
    cut, guess = lax.optimization_barrier((cut, guess))
    return lax.psum_scatter(cut, "mp", scatter_dimension=0, tiled=True), guess


def gathered(mp, part):
    groups = [list(range(0, mp, 2)), list(range(mp - 1, 0, -2))]
    return lax.all_gather(part, "mp", axis_index_groups=groups, axis=0, tiled=True)


def image_by_model(sizes, gram, guess):
    mp, trow, y = sizes["zk"] * sizes["zb"], sizes["trow"], sizes["y"]
    tile = gram[0]
    rows, cols = tile.shape
    own = guess.shape[0]
    flipped = transposed(guess, sizes)
    over_mp = spread(flipped, MP, mp)
    over_mp = over_mp.transpose(1, 0, 2, 3).reshape(2 * mp * own, cols)
    block = spread(over_mp, "trow", trow).reshape(trow, 2, mp * own, cols)
    given = dot(block[:, 1].reshape(trow * mp * own, cols), tile, 1, 1)
    given = lax.ppermute(given, "core", [(0, 1), (1, 0)])
    terms = dot(block[:, 0].reshape(trow * mp * own, cols), tile, 1, 1) + given
    return exchange(terms.reshape(y, mp * own, rows), "y").sum(0)


def shards(sizes, total, terms, rhs, guess):
    zk, zb, trow, y = sizes["zk"], sizes["zb"], sizes["trow"], sizes["y"]
    mp, tcol = zk * zb, y * sizes["core"]
    part_rows, cols = total.shape
    rows = part_rows * zb
    own = rhs.shape[0]
    half = lax.axis_index("zb")
    swap = [(0, 1), (1, 0)]

    def halves(vector):
        low, high = vector[:, :part_rows], vector[:, part_rows:]
        return jnp.where(half == 0, low, high), jnp.where(half == 0, high, low)

    kept, given = halves(rhs)
    near = jnp.concatenate(ordered(half, kept, lax.ppermute(given, "zb", swap)))
    terms = terms.reshape(zk, zb * own, zb, part_rows).transpose(0, 2, 1, 3)
    terms = exchange(terms.reshape(mp, zb * own, part_rows), MP).sum(0)
    near = near - terms

    wide = spread(near, TCOL, tcol).reshape(tcol * zb * own, part_rows)
    second = spread(dot(wide, total, 1, 0), SHARD, trow * zb).sum(0)
    terms = dot(second, total, 1, 1)
    pieces = jnp.concatenate([terms, second], axis=1).reshape(tcol, zb * own, part_rows + cols)
    pieces = exchange(pieces, TCOL)
    third = pieces[:, :, :part_rows].sum(0)
    second = lax.dynamic_slice(
        pieces, (2 * lax.axis_index("trow"), 0, part_rows), (2, zb * own, cols)
    )
    second = jnp.concatenate([second[0], second[1]], axis=1)

    def inner(u, v):
        return jnp.sum(u * v, axis=1, keepdims=True)

    def inverse(x):
        return jnp.where(x > 0, 1.0 / jnp.where(x > 0, x, 1.0), 0.0)

    here, _ = halves(second)
    f0 = jnp.sqrt(inner(near, near))
    e0 = near * inverse(f0)
    s0 = inner(e0, here)
    rest = here - s0 * e0
    s1 = jnp.sqrt(inner(rest, rest))
    e1 = rest * inverse(s1)
    t0 = inner(e0, third)
    t1 = inner(e1, third - t0 * e0)
    numbers = jnp.pad(jnp.concatenate([f0, s0, s1, t0, t1], axis=1), ((0, 0), (0, 123)))
    known = jnp.concatenate([near, third, numbers], axis=1)
    pieces = jnp.broadcast_to(known[None], (trow,) + known.shape)
    pieces = exchange(pieces.reshape(trow * zb, own, known.shape[1]), SHARD)
    f0, s0, s1, t0, t1 = (pieces[:, :, rows + n : rows + n + 1] for n in range(5))
    pair = lax.dynamic_slice(pieces, (zb * lax.axis_index("trow"), 0, 0), (zb, own, rows))
    first = jnp.concatenate([pair[0, :, :part_rows], pair[1, :, :part_rows]], axis=1)
    third = jnp.concatenate([pair[0, :, part_rows:], pair[1, :, part_rows:]], axis=1)
    second = jnp.where(half == 0, second[:own], second[own:])

    norm_first = jnp.sum(f0 * f0, 0)
    alpha = norm_first / jnp.sum(f0 * s0, 0)
    r0, r1 = f0 - alpha * s0, -alpha * s1
    norm_next = jnp.sum(r0 * r0 + r1 * r1, 0)
    beta = norm_next / norm_first
    d0, d1 = r0 + beta * f0, r1
    i0, i1 = s0 - alpha * t0 + beta * s0, s1 - alpha * t1 + beta * s1
    alpha_next = norm_next / jnp.sum(d0 * i0 + d1 * i1, 0)

    residual = first - alpha * second
    direction = residual + beta * first
    image = second - alpha * third + beta * second
    merged = guess + alpha * first + alpha_next * direction
    return merged, residual - alpha_next * image


def solution(mesh):
    mp, trow, tcol = (mesh.shape[a] for a in ("mp", "trow", "tcol"))
    sizes = {"zk": mp // 2, "zb": 2, "trow": trow, "y": tcol // 2, "core": 2}
    split = Mesh(mesh.devices.reshape(tuple(sizes.values())), tuple(sizes))
    every = ("mp", "trow", "tcol")

    def run(function, where, out, *args):
        axes = every if where is mesh else MP + PLANE
        own = axes[0] if where is mesh else MP
        columns = axes[-1:] if where is mesh else TCOL
        spec = {
            "tile": P(own, "trow", columns),
            "row": P((own,) + columns if where is mesh else MP + TCOL, "trow"),
            "block": P(axes),
        }
        return jax.shard_map(
            function,
            mesh=where,
            in_specs=tuple(spec[kind] for kind, _ in args),
            out_specs=tuple(spec[kind] for kind in out),
            check_vma=False,
        )(*(value for _, value in args))

    def whole(gram, rhs, guess):
        part, early = run(
            lambda gram, guess: reduced(mp, gram, guess),
            mesh, ("block", "row"), ("tile", gram), ("row", guess),
        )
        (terms,) = run(
            lambda gram, guess: (image_by_model(sizes, gram, guess),),
            split, ("block",), ("tile", gram), ("row", early),
        )
        part, _ = lax.optimization_barrier((part, terms))
        (total,) = run(lambda part: (gathered(mp, part),), mesh, ("block",), ("block", part))
        return run(
            lambda *args: shards(sizes, *args),
            split, ("row", "row"), ("block", total), ("block", terms), ("row", rhs), ("row", guess),
        )

    return whole
```

```python
import jax
import jax.numpy as jnp
from jax import lax
from jax.sharding import Mesh, PartitionSpec as P

MP = ("zh", "zl")
TCOL = ("y", "core")
PLANE = ("trow",) + TCOL
COPIES = ("zl", "core")
GROUP = ("zh", "y")
HIGHEST = lax.Precision.HIGHEST


def dot(lhs, rhs, lhs_dim, rhs_dim):
    return lax.dot_general(
        lhs,
        rhs,
        (((lhs_dim,), (rhs_dim,)), ((), ())),
        precision=HIGHEST,
        preferred_element_type=jnp.float32,
    )


def exchange(pieces, axes):
    return lax.all_to_all(pieces, axes, 0, 0, tiled=True)


def spread(block, axes, count):
    return exchange(jnp.broadcast_to(block[None], (count,) + block.shape), axes)


def transposed(vector, sizes):
    trow, tcol = sizes["trow"], sizes["y"] * sizes["core"]
    half = vector.shape[1] // 2
    core = lax.axis_index("core")
    halves = (vector[:, :half], vector[:, half:])
    got = []
    for turn in range(2):
        pairs = []
        for i in range(trow):
            for j in range(tcol):
                q, h = j // 2, j % 2
                pairs.append((i * tcol + j, q * tcol + 2 * i + (h ^ turn)))
        sent = jnp.where(core == turn, halves[0], halves[1])
        got.append(lax.ppermute(sent, PLANE, pairs))
    return jnp.stack(got)


def shards(sizes, gram, rhs, guess):
    zh, zl, trow, y, core = sizes.values()
    mp, tcol = zh * zl, y * core
    tile = gram[0]
    rows, cols = tile.shape
    own = rhs.shape[0]
    tall, thin = rows // zl, cols // zh
    group = zh * y

    cut = tile.reshape(zl, tall, zh, thin).transpose(2, 0, 1, 3).reshape(mp * tall, thin)
    cut, guess_after = lax.optimization_barrier((cut, guess))
    part = lax.psum_scatter(cut, MP, scatter_dimension=0, tiled=True)

    flipped = transposed(guess_after, sizes)
    over_mp = spread(flipped, MP, mp)
    over_mp = over_mp.transpose(1, 0, 2, 3).reshape(2 * mp * own, cols)
    block = spread(over_mp, "trow", trow).reshape(trow, 2, mp * own, cols)
    given = dot(block[:, 1].reshape(trow * mp * own, cols), tile, 1, 1)
    given = lax.ppermute(given, "core", [(0, 1), (1, 0)])
    terms = dot(block[:, 0].reshape(trow * mp * own, cols), tile, 1, 1) + given
    terms = exchange(terms.reshape(y, mp * own, rows), "y").sum(0)
    part, _ = lax.optimization_barrier((part, terms))
    terms = exchange(terms.reshape(mp, own, rows), MP).sum(0)
    first = rhs - terms

    total = lax.all_gather(part, COPIES, axis=0, tiled=True).reshape(zl, core, tall, thin)
    total = total.transpose(0, 2, 1, 3).reshape(rows, core * thin)

    wide = spread(first, GROUP, group).reshape(group * own, rows)
    second = spread(dot(wide, total, 1, 0), "trow", trow).sum(0)
    terms = dot(second, total, 1, 1)
    pieces = jnp.concatenate([terms, second], axis=1).reshape(group, own, rows + core * thin)
    pieces = exchange(pieces, GROUP)
    third = pieces[:, :, :rows].sum(0)
    second = pieces[:, :, rows:].reshape(zh, y, own, core, thin)
    second = lax.dynamic_index_in_dim(second, lax.axis_index("trow"), 1, keepdims=False)
    second = second.transpose(1, 2, 0, 3).reshape(own, rows)

    def inner(u, v):
        return jnp.sum(u * v, axis=1, keepdims=True)

    def inverse(x):
        return jnp.where(x > 0, 1.0 / jnp.where(x > 0, x, 1.0), 0.0)

    f0 = jnp.sqrt(inner(first, first))
    e0 = first * inverse(f0)
    s0 = inner(e0, second)
    rest = second - s0 * e0
    s1 = jnp.sqrt(inner(rest, rest))
    e1 = rest * inverse(s1)
    t0 = inner(e0, third)
    t1 = inner(e1, third - t0 * e0)
    known = spread(jnp.concatenate([f0, s0, s1, t0, t1], axis=1), "trow", trow)
    f0, s0, s1, t0, t1 = (known[:, :, n : n + 1] for n in range(5))

    norm_first = jnp.sum(f0 * f0, 0)
    alpha = norm_first / jnp.sum(f0 * s0, 0)
    r0, r1 = f0 - alpha * s0, -alpha * s1
    norm_next = jnp.sum(r0 * r0 + r1 * r1, 0)
    beta = norm_next / norm_first
    d0, d1 = r0 + beta * f0, r1
    i0, i1 = s0 - alpha * t0 + beta * s0, s1 - alpha * t1 + beta * s1
    alpha_next = norm_next / jnp.sum(d0 * i0 + d1 * i1, 0)

    residual = first - alpha * second
    direction = residual + beta * first
    image = second - alpha * third + beta * second
    merged = guess + alpha * first + alpha_next * direction
    return merged, residual - alpha_next * image


def solution(mesh):
    mp, trow, tcol = (mesh.shape[a] for a in ("mp", "trow", "tcol"))
    zl = 4 if mp > 4 else 2
    sizes = {"zh": mp // zl, "zl": zl, "trow": trow, "y": tcol // 2, "core": 2}
    split = Mesh(mesh.devices.reshape(tuple(sizes.values())), tuple(sizes))
    gram_spec = P(MP, "trow", TCOL)
    spec = P(MP + TCOL, "trow")

    def body(gram, rhs, guess):
        return shards(sizes, gram, rhs, guess)

    return jax.shard_map(
        body,
        mesh=split,
        in_specs=(gram_spec, spec, spec),
        out_specs=(spec, spec),
        check_vma=False,
    )
```

```python
import jax
import jax.numpy as jnp
from jax import lax
from jax.experimental import pallas as pl
from jax.experimental.pallas import tpu as pltpu
from jax.sharding import Mesh, PartitionSpec as P

TCOL = ("y", "core")
PLANE = ("trow",) + TCOL
HIGHEST = lax.Precision.HIGHEST


def dot(lhs, rhs, lhs_dim, rhs_dim):
    return lax.dot_general(
        lhs,
        rhs,
        (((lhs_dim,), (rhs_dim,)), ((), ())),
        precision=HIGHEST,
        preferred_element_type=jnp.float32,
    )


def exchange(pieces, axes):
    return lax.all_to_all(pieces, axes, 0, 0, tiled=True)


def spread(block, axes, count):
    return exchange(jnp.broadcast_to(block[None], (count,) + block.shape), axes)


def transposed(vector, sizes):
    trow, tcol = sizes["trow"], sizes["y"] * sizes["core"]
    half = vector.shape[1] // 2
    core = lax.axis_index("core")
    halves = (vector[:, :half], vector[:, half:])
    got = []
    for turn in range(2):
        pairs = []
        for i in range(trow):
            for j in range(tcol):
                q, h = j // 2, j % 2
                pairs.append((i * tcol + j, q * tcol + 2 * i + (h ^ turn)))
        sent = jnp.where(core == turn, halves[0], halves[1])
        got.append(lax.ppermute(sent, PLANE, pairs))
    return jnp.stack(got)


def both_images(first, total, trow):
    blocks, part, cols = total.shape
    _, count, wide = first.shape
    each = wide // cols

    def body(first_ref, total_ref, second_ref, third_ref):
        second = jnp.zeros((count, part), jnp.float32)
        for n in range(blocks):
            x, at = n // each, n % each * cols
            second += dot(first_ref[x, :, at : at + cols], total_ref[n], 1, 1)
        second_ref[...] = second
        for n in range(blocks):
            x, at = n // each, n % each * cols
            third_ref[x, :, at : at + cols] = dot(second, total_ref[n], 1, 0)

    return pl.pallas_call(
        body,
        out_shape=(
            jax.ShapeDtypeStruct((count, part), jnp.float32),
            jax.ShapeDtypeStruct(first.shape, jnp.float32),
        ),
        in_specs=[pl.BlockSpec(memory_space=pltpu.VMEM)] * 2,
        out_specs=(pl.BlockSpec(memory_space=pltpu.VMEM),) * 2,
        cost_estimate=pl.CostEstimate(
            flops=4 * count * total.size, bytes_accessed=4 * (total.size + 2 * first.size), transcendentals=0
        ),
        compiler_params=pltpu.CompilerParams(vmem_limit_bytes=16 * 2**20),
    )(first, total)


def shards(sizes, gram, rhs, guess):
    mp, trow, y, core = sizes.values()
    tcol = y * core
    tile = gram[0]
    rows, cols = tile.shape
    own = rhs.shape[0]
    share = rows // mp

    part = lax.psum_scatter(tile, "mp", scatter_dimension=0, tiled=True)

    over_mp = lax.all_gather(transposed(guess, sizes), "mp", axis=0)
    over_mp = over_mp.transpose(1, 0, 2, 3).reshape(2 * mp * own, cols)
    block = spread(over_mp, "trow", trow).reshape(trow, 2, mp * own, cols)
    given = dot(block[:, 1].reshape(trow * mp * own, cols), tile, 1, 1)
    given = lax.ppermute(given, "core", [(0, 1), (1, 0)])
    terms = dot(block[:, 0].reshape(trow * mp * own, cols), tile, 1, 1) + given
    terms = exchange(terms.reshape(y, mp * own, rows), "y").sum(0)
    terms = exchange(terms.reshape(mp, own, rows), "mp").sum(0)
    first = rhs - terms

    part, _ = lax.optimization_barrier((part, first))
    total = lax.all_gather(part, TCOL, axis=0)

    wide = lax.all_gather(first, "mp", axis=0).reshape(mp * own, rows)
    second, terms = both_images(spread(wide, "trow", trow), total, trow)
    terms = exchange(terms, "trow").sum(0)
    pieces = jnp.concatenate([terms, second], axis=1).reshape(mp, own, rows + share)
    pieces = exchange(pieces, "mp")
    third = pieces[:, :, :rows].sum(0)
    second = pieces[:, :, rows:].transpose(1, 0, 2).reshape(own, rows)

    def inner(u, v):
        return jnp.sum(u * v, axis=1, keepdims=True)

    def inverse(x):
        return jnp.where(x > 0, 1.0 / jnp.where(x > 0, x, 1.0), 0.0)

    f0 = jnp.sqrt(inner(first, first))
    e0 = first * inverse(f0)
    s0 = inner(e0, second)
    rest = second - s0 * e0
    s1 = jnp.sqrt(inner(rest, rest))
    e1 = rest * inverse(s1)
    t0 = inner(e0, third)
    t1 = inner(e1, third - t0 * e0)
    known = spread(jnp.concatenate([f0, s0, s1, t0, t1], axis=1), "trow", trow)
    f0, s0, s1, t0, t1 = (known[:, :, n : n + 1] for n in range(5))

    norm_first = jnp.sum(f0 * f0, 0)
    alpha = norm_first / jnp.sum(f0 * s0, 0)
    r0, r1 = f0 - alpha * s0, -alpha * s1
    norm_next = jnp.sum(r0 * r0 + r1 * r1, 0)
    beta = norm_next / norm_first
    d0, d1 = r0 + beta * f0, r1
    i0, i1 = s0 - alpha * t0 + beta * s0, s1 - alpha * t1 + beta * s1
    alpha_next = norm_next / jnp.sum(d0 * i0 + d1 * i1, 0)

    residual = first - alpha * second
    direction = residual + beta * first
    image = second - alpha * third + beta * second
    merged = guess + alpha * first + alpha_next * direction
    return merged, residual - alpha_next * image


def solution(mesh):
    mp, trow, tcol = (mesh.shape[a] for a in ("mp", "trow", "tcol"))
    sizes = {"mp": mp, "trow": trow, "y": tcol // 2, "core": 2}
    split = Mesh(mesh.devices.reshape(tuple(sizes.values())), tuple(sizes))
    gram_spec = P("mp", "trow", TCOL)
    spec = P(("mp",) + TCOL, "trow")

    def body(gram, rhs, guess):
        return shards(sizes, gram, rhs, guess)

    return jax.shard_map(
        body,
        mesh=split,
        in_specs=(gram_spec, spec, spec),
        out_specs=(spec, spec),
        check_vma=False,
    )
```

```python
import jax
import jax.numpy as jnp
from jax import lax
from jax.experimental import pallas as pl
from jax.experimental.pallas import tpu as pltpu
from jax.sharding import Mesh, PartitionSpec as P

TCOL = ("y", "core")
PLANE = ("trow",) + TCOL
HIGHEST = lax.Precision.HIGHEST


def dot(lhs, rhs, lhs_dim, rhs_dim):
    return lax.dot_general(
        lhs,
        rhs,
        (((lhs_dim,), (rhs_dim,)), ((), ())),
        precision=HIGHEST,
        preferred_element_type=jnp.float32,
    )


def exchange(pieces, axes):
    return lax.all_to_all(pieces, axes, 0, 0, tiled=True)


def spread(block, axes, count):
    return exchange(jnp.broadcast_to(block[None], (count,) + block.shape), axes)


def transposed(vector, sizes):
    trow, tcol = sizes["trow"], sizes["y"] * sizes["core"]
    half = vector.shape[1] // 2
    core = lax.axis_index("core")
    halves = (vector[:, :half], vector[:, half:])
    got = []
    for turn in range(2):
        pairs = []
        for i in range(trow):
            for j in range(tcol):
                q, h = j // 2, j % 2
                pairs.append((i * tcol + j, q * tcol + 2 * i + (h ^ turn)))
        sent = jnp.where(core == turn, halves[0], halves[1])
        got.append(lax.ppermute(sent, PLANE, pairs))
    return jnp.stack(got)


def both_images(first, total, trow):
    blocks, part, cols = total.shape
    _, count, wide = first.shape
    each = wide // cols

    def body(first_ref, total_ref, second_ref, third_ref):
        second = jnp.zeros((count, part), jnp.float32)
        for n in range(blocks):
            x, at = n // each, n % each * cols
            second += dot(first_ref[x, :, at : at + cols], total_ref[n], 1, 1)
        second_ref[...] = second
        for n in range(blocks):
            x, at = n // each, n % each * cols
            third_ref[x, :, at : at + cols] = dot(second, total_ref[n], 1, 0)

    return pl.pallas_call(
        body,
        out_shape=(
            jax.ShapeDtypeStruct((count, part), jnp.float32),
            jax.ShapeDtypeStruct(first.shape, jnp.float32),
        ),
        in_specs=[pl.BlockSpec(memory_space=pltpu.VMEM)] * 2,
        out_specs=(pl.BlockSpec(memory_space=pltpu.VMEM),) * 2,
        cost_estimate=pl.CostEstimate(
            flops=4 * count * total.size, bytes_accessed=4 * (total.size + 2 * first.size), transcendentals=0
        ),
        compiler_params=pltpu.CompilerParams(vmem_limit_bytes=16 * 2**20),
    )(first, total)


def shards(sizes, gram, rhs, guess):
    mp, trow, y, core = sizes.values()
    tcol = y * core
    tile = gram[0]
    rows, cols = tile.shape
    own = rhs.shape[0]
    share = rows // mp

    part = lax.psum_scatter(tile, "mp", scatter_dimension=0, tiled=True)

    over_mp = spread(transposed(guess, sizes), "mp", mp)
    over_mp = over_mp.transpose(1, 0, 2, 3).reshape(2 * mp * own, cols)
    block = spread(over_mp, "trow", trow).reshape(trow, 2, mp * own, cols)
    given = dot(block[:, 1].reshape(trow * mp * own, cols), tile, 1, 1)
    given = lax.ppermute(given, "core", [(0, 1), (1, 0)])
    terms = dot(block[:, 0].reshape(trow * mp * own, cols), tile, 1, 1) + given
    terms = exchange(terms.reshape(y, mp * own, rows), "y").sum(0)
    terms = exchange(terms.reshape(mp, own, rows), "mp").sum(0)
    first = rhs - terms

    part, _ = lax.optimization_barrier((part, first))
    total = lax.all_gather(part, TCOL, axis=0)

    wide = spread(first, "mp", mp).reshape(mp * own, rows)
    second, terms = both_images(spread(wide, "trow", trow), total, trow)
    terms = exchange(terms, "trow").sum(0)
    pieces = jnp.concatenate([terms, second], axis=1).reshape(mp, own, rows + share)
    pieces = exchange(pieces, "mp")
    third = pieces[:, :, :rows].sum(0)
    second = pieces[:, :, rows:].transpose(1, 0, 2).reshape(own, rows)

    def inner(u, v):
        return jnp.sum(u * v, axis=1, keepdims=True)

    def inverse(x):
        return jnp.where(x > 0, 1.0 / jnp.where(x > 0, x, 1.0), 0.0)

    f0 = jnp.sqrt(inner(first, first))
    e0 = first * inverse(f0)
    s0 = inner(e0, second)
    rest = second - s0 * e0
    s1 = jnp.sqrt(inner(rest, rest))
    e1 = rest * inverse(s1)
    t0 = inner(e0, third)
    t1 = inner(e1, third - t0 * e0)
    known = spread(jnp.concatenate([f0, s0, s1, t0, t1], axis=1), "trow", trow)
    f0, s0, s1, t0, t1 = (known[:, :, n : n + 1] for n in range(5))

    norm_first = jnp.sum(f0 * f0, 0)
    alpha = norm_first / jnp.sum(f0 * s0, 0)
    r0, r1 = f0 - alpha * s0, -alpha * s1
    norm_next = jnp.sum(r0 * r0 + r1 * r1, 0)
    beta = norm_next / norm_first
    d0, d1 = r0 + beta * f0, r1
    i0, i1 = s0 - alpha * t0 + beta * s0, s1 - alpha * t1 + beta * s1
    alpha_next = norm_next / jnp.sum(d0 * i0 + d1 * i1, 0)

    residual = first - alpha * second
    direction = residual + beta * first
    image = second - alpha * third + beta * second
    merged = guess + alpha * first + alpha_next * direction
    return merged, residual - alpha_next * image


def solution(mesh):
    mp, trow, tcol = (mesh.shape[a] for a in ("mp", "trow", "tcol"))
    sizes = {"mp": mp, "trow": trow, "y": tcol // 2, "core": 2}
    split = Mesh(mesh.devices.reshape(tuple(sizes.values())), tuple(sizes))
    gram_spec = P("mp", "trow", TCOL)
    spec = P(("mp",) + TCOL, "trow")

    def body(gram, rhs, guess):
        return shards(sizes, gram, rhs, guess)

    return jax.shard_map(
        body,
        mesh=split,
        in_specs=(gram_spec, spec, spec),
        out_specs=(spec, spec),
        check_vma=False,
    )
```

```python
import jax
import jax.numpy as jnp
from jax import lax
from jax.experimental import pallas as pl
from jax.experimental.pallas import tpu as pltpu
from jax.sharding import Mesh, PartitionSpec as P

TCOL = ("y", "core")
PLANE = ("trow",) + TCOL
HIGHEST = lax.Precision.HIGHEST


def dot(lhs, rhs, lhs_dim, rhs_dim):
    return lax.dot_general(
        lhs,
        rhs,
        (((lhs_dim,), (rhs_dim,)), ((), ())),
        precision=HIGHEST,
        preferred_element_type=jnp.float32,
    )


def exchange(pieces, axes):
    return lax.all_to_all(pieces, axes, 0, 0, tiled=True)


def spread(block, axes, count):
    return exchange(jnp.broadcast_to(block[None], (count,) + block.shape), axes)


def transposed(vector, sizes):
    trow, tcol = sizes["trow"], sizes["y"] * sizes["core"]
    half = vector.shape[1] // 2
    core = lax.axis_index("core")
    halves = (vector[:, :half], vector[:, half:])
    got = []
    for turn in range(2):
        pairs = []
        for i in range(trow):
            for j in range(tcol):
                q, h = j // 2, j % 2
                pairs.append((i * tcol + j, q * tcol + 2 * i + (h ^ turn)))
        sent = jnp.where(core == turn, halves[0], halves[1])
        got.append(lax.ppermute(sent, PLANE, pairs))
    return jnp.stack(got)


def vmem_call(body, out_shape, flops, *args):
    place = pl.BlockSpec(memory_space=pltpu.VMEM)
    moved = 4 * sum(arg.size for arg in args) + 4 * out_shape.size
    return pl.pallas_call(
        body,
        out_shape=out_shape,
        in_specs=[place] * len(args),
        out_specs=place,
        cost_estimate=pl.CostEstimate(flops=flops, bytes_accessed=moved, transcendentals=0),
        compiler_params=pltpu.CompilerParams(vmem_limit_bytes=16 * 2**20),
    )(*args)


def partial_second(first, total, copies):
    count, part = first.shape[0], total.shape[0]

    def body(first_ref, total_ref, out_ref):
        second = dot(first_ref[...], total_ref[...], 1, 1)
        for n in range(copies):
            out_ref[n] = second

    out = jax.ShapeDtypeStruct((copies, count, part), jnp.float32)
    return vmem_call(body, out, 2 * count * total.size, first, total)


def partial_third(shares, total, pieces):
    count, part = shares.shape[1:]
    rows = total.shape[1]
    own = count // pieces

    def body(shares_ref, total_ref, out_ref):
        second = shares_ref[0]
        for n in range(1, shares.shape[0]):
            second += shares_ref[n]
        third = dot(second, total_ref[...], 1, 0)
        for n in range(pieces):
            out_ref[n, :, :rows] = third[n * own : (n + 1) * own]
            out_ref[n, :, rows:] = second[n * own : (n + 1) * own]

    out = jax.ShapeDtypeStruct((pieces, own, rows + part), jnp.float32)
    return vmem_call(body, out, 2 * count * total.size, shares, total)


def shards(sizes, gram, rhs, guess):
    mp, trow, y, core = sizes.values()
    tcol = y * core
    tile = gram[0]
    rows, cols = tile.shape
    own = rhs.shape[0]
    share = cols // mp

    part = lax.psum_scatter(tile.T, "mp", scatter_dimension=0, tiled=True)

    over_mp = spread(transposed(guess, sizes), "mp", mp)
    over_mp = over_mp.transpose(1, 0, 2, 3).reshape(2 * mp * own, cols)
    block = spread(over_mp, "trow", trow).reshape(trow, 2, mp * own, cols)
    given = dot(block[:, 1].reshape(trow * mp * own, cols), tile, 1, 1)
    given = lax.ppermute(given, "core", [(0, 1), (1, 0)])
    terms = dot(block[:, 0].reshape(trow * mp * own, cols), tile, 1, 1) + given
    terms = exchange(terms.reshape(y, mp * own, rows), "y").sum(0)
    part, _ = lax.optimization_barrier((part, terms))
    terms = exchange(terms.reshape(mp, own, rows), "mp").sum(0)
    first = rhs - terms

    total = lax.all_gather(part, TCOL, axis=0, tiled=True)

    wide = spread(first, "mp", mp).reshape(mp * own, rows)
    shares = exchange(partial_second(wide, total, trow), "trow")
    pieces = exchange(partial_third(shares, total, mp), "mp")
    third = pieces[:, :, :rows].sum(0)
    second = pieces[:, :, rows:].reshape(mp, own, trow, core, share)
    second = lax.dynamic_index_in_dim(second, lax.axis_index("trow"), 2, keepdims=False)
    second = second.transpose(1, 2, 0, 3).reshape(own, rows)

    def inner(u, v):
        return jnp.sum(u * v, axis=1, keepdims=True)

    def inverse(x):
        return jnp.where(x > 0, 1.0 / jnp.where(x > 0, x, 1.0), 0.0)

    f0 = jnp.sqrt(inner(first, first))
    e0 = first * inverse(f0)
    s0 = inner(e0, second)
    rest = second - s0 * e0
    s1 = jnp.sqrt(inner(rest, rest))
    e1 = rest * inverse(s1)
    t0 = inner(e0, third)
    t1 = inner(e1, third - t0 * e0)
    known = spread(jnp.concatenate([f0, s0, s1, t0, t1], axis=1), "trow", trow)
    f0, s0, s1, t0, t1 = (known[:, :, n : n + 1] for n in range(5))

    norm_first = jnp.sum(f0 * f0, 0)
    alpha = norm_first / jnp.sum(f0 * s0, 0)
    r0, r1 = f0 - alpha * s0, -alpha * s1
    norm_next = jnp.sum(r0 * r0 + r1 * r1, 0)
    beta = norm_next / norm_first
    d0, d1 = r0 + beta * f0, r1
    i0, i1 = s0 - alpha * t0 + beta * s0, s1 - alpha * t1 + beta * s1
    alpha_next = norm_next / jnp.sum(d0 * i0 + d1 * i1, 0)

    residual = first - alpha * second
    direction = residual + beta * first
    image = second - alpha * third + beta * second
    merged = guess + alpha * first + alpha_next * direction
    return merged, residual - alpha_next * image


def solution(mesh):
    mp, trow, tcol = (mesh.shape[a] for a in ("mp", "trow", "tcol"))
    sizes = {"mp": mp, "trow": trow, "y": tcol // 2, "core": 2}
    split = Mesh(mesh.devices.reshape(tuple(sizes.values())), tuple(sizes))
    gram_spec = P("mp", "trow", TCOL)
    spec = P(("mp",) + TCOL, "trow")

    def body(gram, rhs, guess):
        return shards(sizes, gram, rhs, guess)

    return jax.shard_map(
        body,
        mesh=split,
        in_specs=(gram_spec, spec, spec),
        out_specs=(spec, spec),
        check_vma=False,
    )
```

```python
import jax
import jax.numpy as jnp
from jax import lax
from jax.experimental import pallas as pl
from jax.experimental.pallas import tpu as pltpu
from jax.sharding import Mesh, PartitionSpec as P

TCOL = ("y", "core")
PLANE = ("trow",) + TCOL
HINT = 10**10
HIGHEST = lax.Precision.HIGHEST


def dot(lhs, rhs, lhs_dim, rhs_dim):
    return lax.dot_general(
        lhs,
        rhs,
        (((lhs_dim,), (rhs_dim,)), ((), ())),
        precision=HIGHEST,
        preferred_element_type=jnp.float32,
    )


def exchange(pieces, axes):
    return lax.all_to_all(pieces, axes, 0, 0, tiled=True)


def spread(block, axes, count):
    return exchange(jnp.broadcast_to(block[None], (count,) + block.shape), axes)


def transposed(vector, sizes):
    trow, tcol = sizes["trow"], sizes["y"] * sizes["core"]
    half = vector.shape[1] // 2
    core = lax.axis_index("core")
    halves = (vector[:, :half], vector[:, half:])
    got = []
    for turn in range(2):
        pairs = []
        for i in range(trow):
            for j in range(tcol):
                q, h = j // 2, j % 2
                pairs.append((i * tcol + j, q * tcol + 2 * i + (h ^ turn)))
        sent = jnp.where(core == turn, halves[0], halves[1])
        got.append(lax.ppermute(sent, PLANE, pairs))
    return jnp.stack(got)


def vmem_call(body, out_shape, flops, *args):
    place = pl.BlockSpec(memory_space=pltpu.VMEM)
    outs = jax.tree.leaves(out_shape)
    moved = 4 * sum(array.size for array in list(args) + outs)
    return pl.pallas_call(
        body,
        out_shape=out_shape,
        in_specs=[place] * len(args),
        out_specs=jax.tree.map(lambda _: place, out_shape),
        cost_estimate=pl.CostEstimate(flops=flops, bytes_accessed=moved, transcendentals=0),
        compiler_params=pltpu.CompilerParams(vmem_limit_bytes=16 * 2**20),
    )(*args)


def f32(*shape):
    return jax.ShapeDtypeStruct(shape, jnp.float32)


def remainder(terms, rhs, flops):
    count = terms.shape[0]

    def body(terms_ref, rhs_ref, first_ref, out_ref):
        total = terms_ref[0]
        for n in range(1, count):
            total += terms_ref[n]
        first = rhs_ref[...] - total
        first_ref[...] = first
        for n in range(count):
            out_ref[n] = first

    return vmem_call(body, (f32(*rhs.shape), f32(*terms.shape)), flops, terms, rhs)


def partial_second(first, total, copies):
    count, part = first.shape[0], total.shape[0]

    def body(first_ref, total_ref, out_ref):
        second = dot(first_ref[...], total_ref[...], 1, 1)
        for n in range(copies):
            out_ref[n] = second

    out = f32(copies, count, part)
    return vmem_call(body, out, 2 * count * total.size, first, total)


def partial_third(shares, total, pieces):
    count, part = shares.shape[1:]
    rows = total.shape[1]
    own = count // pieces

    def body(shares_ref, total_ref, out_ref):
        second = shares_ref[0]
        for n in range(1, shares.shape[0]):
            second += shares_ref[n]
        third = dot(second, total_ref[...], 1, 0)
        for n in range(pieces):
            out_ref[n, :, :rows] = third[n * own : (n + 1) * own]
            out_ref[n, :, rows:] = second[n * own : (n + 1) * own]

    out = f32(pieces, own, rows + part)
    return vmem_call(body, out, 2 * count * total.size, shares, total)


def inner(u, v):
    return jnp.sum(u * v, axis=1, keepdims=True)


def inverse(x):
    return jnp.where(x > 0, 1.0 / jnp.where(x > 0, x, 1.0), 0.0)


def coordinates(first, second, pieces, copies):
    own, rows = first.shape

    def body(first_ref, second_ref, pieces_ref, third_ref, out_ref):
        first, second = first_ref[...], second_ref[...]
        third = pieces_ref[0, :, :rows]
        for n in range(1, pieces.shape[0]):
            third += pieces_ref[n, :, :rows]
        third_ref[...] = third
        f0 = jnp.sqrt(inner(first, first))
        e0 = first * inverse(f0)
        s0 = inner(e0, second)
        rest = second - s0 * e0
        s1 = jnp.sqrt(inner(rest, rest))
        e1 = rest * inverse(s1)
        t0 = inner(e0, third)
        t1 = inner(e1, third - t0 * e0)
        lane = lax.broadcasted_iota(jnp.int32, (own, 128), 1)
        packed = jnp.zeros((own, 128), jnp.float32)
        for n, number in enumerate((f0, s0, s1, t0, t1)):
            packed = jnp.where(lane == n, number, packed)
        for n in range(copies):
            out_ref[n] = packed

    return vmem_call(body, (f32(own, rows), f32(copies, own, 128)), pieces.size, first, second, pieces)


def combined(known, guess, first, second, third):
    blocks = known.shape[0]

    def body(known_ref, guess_ref, first_ref, second_ref, third_ref, merged_ref, residual_ref):
        parts = [known_ref[n] for n in range(blocks)]
        f0, s0, s1, t0, t1 = ([part[:, n : n + 1] for part in parts] for n in range(5))

        def total(*products):
            return sum(u * v for us, vs in products for u, v in zip(us, vs))

        norm_first = total((f0, f0))
        alpha = norm_first / total((f0, s0))
        r0 = [f - alpha * s for f, s in zip(f0, s0)]
        r1 = [-alpha * s for s in s1]
        norm_next = total((r0, r0), (r1, r1))
        beta = norm_next / norm_first
        d0 = [r + beta * f for r, f in zip(r0, f0)]
        i0 = [s - alpha * t + beta * s for s, t in zip(s0, t0)]
        i1 = [s - alpha * t + beta * s for s, t in zip(s1, t1)]
        alpha_next = norm_next / total((d0, i0), (r1, i1))

        first, second = first_ref[...], second_ref[...]
        residual = first - alpha * second
        direction = residual + beta * first
        image = second - alpha * third_ref[...] + beta * second
        merged_ref[...] = guess_ref[...] + alpha * first + alpha_next * direction
        residual_ref[...] = residual - alpha_next * image

    out = (f32(*guess.shape), f32(*guess.shape))
    return vmem_call(body, out, 16 * guess.size, known, guess, first, second, third)


def shards(sizes, gram, rhs, guess):
    mp, trow, y, core = sizes.values()
    tcol = y * core
    tile = gram[0]
    rows, cols = tile.shape
    own = rhs.shape[0]
    share = cols // mp

    part = lax.psum_scatter(tile.T, "mp", scatter_dimension=0, tiled=True)

    over_mp = spread(transposed(guess, sizes), "mp", mp)
    over_mp = over_mp.transpose(1, 0, 2, 3).reshape(2 * mp * own, cols)
    block = spread(over_mp, "trow", trow).reshape(trow, 2, mp * own, cols)
    given = dot(block[:, 1].reshape(trow * mp * own, cols), tile, 1, 1)
    given = lax.ppermute(given, "core", [(0, 1), (1, 0)])
    terms = dot(block[:, 0].reshape(trow * mp * own, cols), tile, 1, 1) + given
    terms = exchange(terms.reshape(y, mp * own, rows), "y").sum(0)
    part, _ = lax.optimization_barrier((part, terms))
    terms = exchange(terms.reshape(mp, own, rows), "mp")
    first, copies = remainder(terms, rhs, HINT)

    total = lax.all_gather(part, TCOL, axis=0, tiled=True)

    wide = exchange(copies, "mp").reshape(mp * own, rows)
    shares = exchange(partial_second(wide, total, trow), "trow")
    pieces = exchange(partial_third(shares, total, mp), "mp")
    second = pieces[:, :, rows:].reshape(mp, own, trow, core, share)
    second = lax.dynamic_index_in_dim(second, lax.axis_index("trow"), 2, keepdims=False)
    second = second.transpose(1, 2, 0, 3).reshape(own, rows)
    third, numbers = coordinates(first, second, pieces, trow)
    return combined(exchange(numbers, "trow"), guess, first, second, third)


def solution(mesh):
    mp, trow, tcol = (mesh.shape[a] for a in ("mp", "trow", "tcol"))
    sizes = {"mp": mp, "trow": trow, "y": tcol // 2, "core": 2}
    split = Mesh(mesh.devices.reshape(tuple(sizes.values())), tuple(sizes))
    gram_spec = P("mp", "trow", TCOL)
    spec = P(("mp",) + TCOL, "trow")

    def body(gram, rhs, guess):
        return shards(sizes, gram, rhs, guess)

    return jax.shard_map(
        body,
        mesh=split,
        in_specs=(gram_spec, spec, spec),
        out_specs=(spec, spec),
        check_vma=False,
    )
```

```python
import jax
import jax.numpy as jnp
from jax import lax
from jax.experimental import pallas as pl
from jax.experimental.pallas import tpu as pltpu
from jax.sharding import Mesh, PartitionSpec as P

TCOL = ("y", "core")
PLANE = ("trow",) + TCOL
HIGHEST = lax.Precision.HIGHEST


def dot(lhs, rhs, lhs_dim, rhs_dim):
    return lax.dot_general(
        lhs,
        rhs,
        (((lhs_dim,), (rhs_dim,)), ((), ())),
        precision=HIGHEST,
        preferred_element_type=jnp.float32,
    )


def exchange(pieces, axes):
    return lax.all_to_all(pieces, axes, 0, 0, tiled=True)


def spread(block, axes, count):
    return exchange(jnp.broadcast_to(block[None], (count,) + block.shape), axes)


def transposed(vector, sizes):
    trow, tcol = sizes["trow"], sizes["y"] * sizes["core"]
    half = vector.shape[1] // 2
    core = lax.axis_index("core")
    halves = (vector[:, :half], vector[:, half:])
    got = []
    for turn in range(2):
        pairs = []
        for i in range(trow):
            for j in range(tcol):
                q, h = j // 2, j % 2
                pairs.append((i * tcol + j, q * tcol + 2 * i + (h ^ turn)))
        sent = jnp.where(core == turn, halves[0], halves[1])
        got.append(lax.ppermute(sent, PLANE, pairs))
    return jnp.stack(got)


def vmem_call(body, out_shape, flops, *args):
    place = pl.BlockSpec(memory_space=pltpu.VMEM)
    outs = jax.tree.leaves(out_shape)
    moved = 4 * sum(array.size for array in list(args) + outs)
    return pl.pallas_call(
        body,
        out_shape=out_shape,
        in_specs=[place] * len(args),
        out_specs=jax.tree.map(lambda _: place, out_shape),
        cost_estimate=pl.CostEstimate(flops=flops, bytes_accessed=moved, transcendentals=0),
        compiler_params=pltpu.CompilerParams(vmem_limit_bytes=16 * 2**20),
    )(*args)


def f32(*shape):
    return jax.ShapeDtypeStruct(shape, jnp.float32)


def remainder(terms, rhs):
    count = terms.shape[0]

    def body(terms_ref, rhs_ref, first_ref, out_ref):
        total = terms_ref[0]
        for n in range(1, count):
            total += terms_ref[n]
        first = rhs_ref[...] - total
        first_ref[...] = first
        for n in range(count):
            out_ref[n] = first

    return vmem_call(body, (f32(*rhs.shape), f32(*terms.shape)), terms.size, terms, rhs)


def partial_second(first, total, copies):
    count, part = first.shape[0], total.shape[0]

    def body(first_ref, total_ref, out_ref):
        second = dot(first_ref[...], total_ref[...], 1, 1)
        for n in range(copies):
            out_ref[n] = second

    out = f32(copies, count, part)
    return vmem_call(body, out, 2 * count * total.size, first, total)


def partial_third(shares, total, pieces):
    count, part = shares.shape[1:]
    rows = total.shape[1]
    own = count // pieces

    def body(shares_ref, total_ref, out_ref):
        second = shares_ref[0]
        for n in range(1, shares.shape[0]):
            second += shares_ref[n]
        third = dot(second, total_ref[...], 1, 0)
        for n in range(pieces):
            out_ref[n, :, :rows] = third[n * own : (n + 1) * own]
            out_ref[n, :, rows:] = second[n * own : (n + 1) * own]

    out = f32(pieces, own, rows + part)
    return vmem_call(body, out, 2 * count * total.size, shares, total)


def inner(u, v):
    return jnp.sum(u * v, axis=1, keepdims=True)


def inverse(x):
    return jnp.where(x > 0, 1.0 / jnp.where(x > 0, x, 1.0), 0.0)


def coordinates(first, second, pieces, copies):
    own, rows = first.shape

    def body(first_ref, second_ref, pieces_ref, third_ref, out_ref):
        first, second = first_ref[...], second_ref[...]
        third = pieces_ref[0, :, :rows]
        for n in range(1, pieces.shape[0]):
            third += pieces_ref[n, :, :rows]
        third_ref[...] = third
        f0 = jnp.sqrt(inner(first, first))
        e0 = first * inverse(f0)
        s0 = inner(e0, second)
        rest = second - s0 * e0
        s1 = jnp.sqrt(inner(rest, rest))
        e1 = rest * inverse(s1)
        t0 = inner(e0, third)
        t1 = inner(e1, third - t0 * e0)
        lane = lax.broadcasted_iota(jnp.int32, (own, 128), 1)
        packed = jnp.zeros((own, 128), jnp.float32)
        for n, number in enumerate((f0, s0, s1, t0, t1)):
            packed = jnp.where(lane == n, number, packed)
        for n in range(copies):
            out_ref[n] = packed

    return vmem_call(body, (f32(own, rows), f32(copies, own, 128)), pieces.size, first, second, pieces)


def combined(known, guess, first, second, third):
    blocks = known.shape[0]

    def body(known_ref, guess_ref, first_ref, second_ref, third_ref, merged_ref, residual_ref):
        parts = [known_ref[n] for n in range(blocks)]
        f0, s0, s1, t0, t1 = ([part[:, n : n + 1] for part in parts] for n in range(5))

        def total(*products):
            return sum(u * v for us, vs in products for u, v in zip(us, vs))

        norm_first = total((f0, f0))
        alpha = norm_first / total((f0, s0))
        r0 = [f - alpha * s for f, s in zip(f0, s0)]
        r1 = [-alpha * s for s in s1]
        norm_next = total((r0, r0), (r1, r1))
        beta = norm_next / norm_first
        d0 = [r + beta * f for r, f in zip(r0, f0)]
        i0 = [s - alpha * t + beta * s for s, t in zip(s0, t0)]
        i1 = [s - alpha * t + beta * s for s, t in zip(s1, t1)]
        alpha_next = norm_next / total((d0, i0), (r1, i1))

        first, second = first_ref[...], second_ref[...]
        residual = first - alpha * second
        direction = residual + beta * first
        image = second - alpha * third_ref[...] + beta * second
        merged_ref[...] = guess_ref[...] + alpha * first + alpha_next * direction
        residual_ref[...] = residual - alpha_next * image

    out = (f32(*guess.shape), f32(*guess.shape))
    return vmem_call(body, out, 16 * guess.size, known, guess, first, second, third)


def shards(sizes, gram, rhs, guess):
    mp, trow, y, core = sizes.values()
    tcol = y * core
    tile = gram[0]
    rows, cols = tile.shape
    own = rhs.shape[0]
    share = cols // mp

    part = lax.psum_scatter(tile.T, "mp", scatter_dimension=0, tiled=True)

    over_mp = spread(transposed(guess, sizes), "mp", mp)
    over_mp = over_mp.transpose(1, 0, 2, 3).reshape(2 * mp * own, cols)
    block = spread(over_mp, "trow", trow).reshape(trow, 2, mp * own, cols)
    given = dot(block[:, 1].reshape(trow * mp * own, cols), tile, 1, 1)
    given = lax.ppermute(given, "core", [(0, 1), (1, 0)])
    terms = dot(block[:, 0].reshape(trow * mp * own, cols), tile, 1, 1) + given
    terms = exchange(terms.reshape(y, mp * own, rows), "y").sum(0)
    part, _ = lax.optimization_barrier((part, terms))
    terms = exchange(terms.reshape(mp, own, rows), "mp")
    first, copies = remainder(terms, rhs)

    total = lax.all_gather(part, TCOL, axis=0, tiled=True)

    wide = exchange(copies, "mp").reshape(mp * own, rows)
    shares = exchange(partial_second(wide, total, trow), "trow")
    pieces = exchange(partial_third(shares, total, mp), "mp")
    second = pieces[:, :, rows:].reshape(mp, own, trow, core, share)
    second = lax.dynamic_index_in_dim(second, lax.axis_index("trow"), 2, keepdims=False)
    second = second.transpose(1, 2, 0, 3).reshape(own, rows)
    third, numbers = coordinates(first, second, pieces, trow)
    return combined(exchange(numbers, "trow"), guess, first, second, third)


def solution(mesh):
    mp, trow, tcol = (mesh.shape[a] for a in ("mp", "trow", "tcol"))
    sizes = {"mp": mp, "trow": trow, "y": tcol // 2, "core": 2}
    split = Mesh(mesh.devices.reshape(tuple(sizes.values())), tuple(sizes))
    gram_spec = P("mp", "trow", TCOL)
    spec = P(("mp",) + TCOL, "trow")

    def body(gram, rhs, guess):
        return shards(sizes, gram, rhs, guess)

    return jax.shard_map(
        body,
        mesh=split,
        in_specs=(gram_spec, spec, spec),
        out_specs=(spec, spec),
        check_vma=False,
    )
```

```python
import jax
import jax.numpy as jnp
from jax import lax
from jax.experimental import pallas as pl
from jax.experimental.pallas import tpu as pltpu
from jax.sharding import Mesh, PartitionSpec as P

TCOL = ("y", "core")
PLANE = ("trow",) + TCOL
HIGHEST = lax.Precision.HIGHEST


def dot(lhs, rhs, lhs_dim, rhs_dim):
    return lax.dot_general(
        lhs,
        rhs,
        (((lhs_dim,), (rhs_dim,)), ((), ())),
        precision=HIGHEST,
        preferred_element_type=jnp.float32,
    )


def exchange(pieces, axes):
    return lax.all_to_all(pieces, axes, 0, 0, tiled=True)


def spread(block, axes, count):
    return exchange(jnp.broadcast_to(block[None], (count,) + block.shape), axes)


def transposed(vector, sizes):
    trow, tcol = sizes["trow"], sizes["y"] * sizes["core"]
    half = vector.shape[1] // 2
    core = lax.axis_index("core")
    halves = (vector[:, :half], vector[:, half:])
    got = []
    for turn in range(2):
        pairs = []
        for i in range(trow):
            for j in range(tcol):
                q, h = j // 2, j % 2
                pairs.append((i * tcol + j, q * tcol + 2 * i + (h ^ turn)))
        sent = jnp.where(core == turn, halves[0], halves[1])
        got.append(lax.ppermute(sent, PLANE, pairs))
    return jnp.stack(got)


def vmem_call(body, out_shape, flops, *args):
    place = pl.BlockSpec(memory_space=pltpu.VMEM)
    outs = jax.tree.leaves(out_shape)
    moved = 4 * sum(array.size for array in list(args) + outs)
    return pl.pallas_call(
        body,
        out_shape=out_shape,
        in_specs=[place] * len(args),
        out_specs=jax.tree.map(lambda _: place, out_shape),
        cost_estimate=pl.CostEstimate(flops=flops, bytes_accessed=moved, transcendentals=0),
        compiler_params=pltpu.CompilerParams(vmem_limit_bytes=16 * 2**20),
    )(*args)


def f32(*shape):
    return jax.ShapeDtypeStruct(shape, jnp.float32)


def remainder(terms, rhs):
    count = terms.shape[0]

    def body(terms_ref, rhs_ref, first_ref, out_ref):
        total = terms_ref[0]
        for n in range(1, count):
            total += terms_ref[n]
        first = rhs_ref[...] - total
        first_ref[...] = first
        for n in range(count):
            out_ref[n] = first

    return vmem_call(body, (f32(*rhs.shape), f32(*terms.shape)), terms.size, terms, rhs)


def partial_second(first, total, copies):
    count, part = first.shape[0], total.shape[0]

    def body(first_ref, total_ref, out_ref):
        second = dot(first_ref[...], total_ref[...], 1, 1)
        for n in range(copies):
            out_ref[n] = second

    out = f32(copies, count, part)
    return vmem_call(body, out, 2 * count * total.size, first, total)


def partial_third(shares, total, pieces, trow, blocks):
    count, part = shares.shape[1:]
    rows = total.shape[1]
    own, near = count // pieces, part // blocks

    def body(shares_ref, total_ref, trow_ref, out_ref):
        second = shares_ref[0]
        for n in range(1, shares.shape[0]):
            second += shares_ref[n]
        third = dot(second, total_ref[...], 1, 0)
        block = second[:, :near]
        for n in range(1, blocks):
            block = jnp.where(trow_ref[0] == n, second[:, n * near : (n + 1) * near], block)
        for n in range(pieces):
            out_ref[n, :, :rows] = third[n * own : (n + 1) * own]
            out_ref[n, :, rows:] = block[n * own : (n + 1) * own]

    place = pl.BlockSpec(memory_space=pltpu.VMEM)
    return pl.pallas_call(
        body,
        out_shape=f32(pieces, own, rows + near),
        in_specs=[place, place, pl.BlockSpec(memory_space=pltpu.SMEM)],
        out_specs=place,
        cost_estimate=pl.CostEstimate(
            flops=2 * count * total.size, bytes_accessed=4 * total.size, transcendentals=0
        ),
        compiler_params=pltpu.CompilerParams(vmem_limit_bytes=16 * 2**20),
    )(shares, total, trow)


def inner(u, v):
    return jnp.sum(u * v, axis=1, keepdims=True)


def inverse(x):
    return jnp.where(x > 0, 1.0 / jnp.where(x > 0, x, 1.0), 0.0)


def coordinates(first, second, pieces, copies):
    own, rows = first.shape

    def body(first_ref, second_ref, pieces_ref, third_ref, out_ref):
        first, second = first_ref[...], second_ref[...]
        third = pieces_ref[0, :, :rows]
        for n in range(1, pieces.shape[0]):
            third += pieces_ref[n, :, :rows]
        third_ref[...] = third
        f0 = jnp.sqrt(inner(first, first))
        e0 = first * inverse(f0)
        s0 = inner(e0, second)
        rest = second - s0 * e0
        s1 = jnp.sqrt(inner(rest, rest))
        e1 = rest * inverse(s1)
        t0 = inner(e0, third)
        t1 = inner(e1, third - t0 * e0)
        lane = lax.broadcasted_iota(jnp.int32, (own, 128), 1)
        packed = jnp.zeros((own, 128), jnp.float32)
        for n, number in enumerate((f0, s0, s1, t0, t1)):
            packed = jnp.where(lane == n, number, packed)
        for n in range(copies):
            out_ref[n] = packed

    return vmem_call(body, (f32(own, rows), f32(copies, own, 128)), pieces.size, first, second, pieces)


def combined(known, guess, first, second, third):
    blocks = known.shape[0]

    def body(known_ref, guess_ref, first_ref, second_ref, third_ref, merged_ref, residual_ref):
        parts = [known_ref[n] for n in range(blocks)]
        f0, s0, s1, t0, t1 = ([part[:, n : n + 1] for part in parts] for n in range(5))

        def total(*products):
            return sum(u * v for us, vs in products for u, v in zip(us, vs))

        norm_first = total((f0, f0))
        alpha = norm_first / total((f0, s0))
        r0 = [f - alpha * s for f, s in zip(f0, s0)]
        r1 = [-alpha * s for s in s1]
        norm_next = total((r0, r0), (r1, r1))
        beta = norm_next / norm_first
        d0 = [r + beta * f for r, f in zip(r0, f0)]
        i0 = [s - alpha * t + beta * s for s, t in zip(s0, t0)]
        i1 = [s - alpha * t + beta * s for s, t in zip(s1, t1)]
        alpha_next = norm_next / total((d0, i0), (r1, i1))

        first, second = first_ref[...], second_ref[...]
        residual = first - alpha * second
        direction = residual + beta * first
        image = second - alpha * third_ref[...] + beta * second
        merged_ref[...] = guess_ref[...] + alpha * first + alpha_next * direction
        residual_ref[...] = residual - alpha_next * image

    out = (f32(*guess.shape), f32(*guess.shape))
    return vmem_call(body, out, 16 * guess.size, known, guess, first, second, third)


def shards(sizes, gram, rhs, guess):
    mp, trow, y, core = sizes.values()
    tcol = y * core
    tile = gram[0]
    rows, cols = tile.shape
    own = rhs.shape[0]
    share = cols // mp

    part = lax.psum_scatter(tile.T, "mp", scatter_dimension=0, tiled=True)

    at, early = lax.optimization_barrier((lax.axis_index("trow").reshape(1), guess))
    over_mp = spread(transposed(early, sizes), "mp", mp)
    over_mp = over_mp.transpose(1, 0, 2, 3).reshape(2 * mp * own, cols)
    block = spread(over_mp, "trow", trow).reshape(trow, 2, mp * own, cols)
    given = dot(block[:, 1].reshape(trow * mp * own, cols), tile, 1, 1)
    given = lax.ppermute(given, "core", [(0, 1), (1, 0)])
    terms = dot(block[:, 0].reshape(trow * mp * own, cols), tile, 1, 1) + given
    terms = exchange(terms.reshape(y, mp * own, rows), "y").sum(0)
    part, _ = lax.optimization_barrier((part, terms))
    terms = exchange(terms.reshape(mp, own, rows), "mp")
    first, copies = remainder(terms, rhs)

    total = lax.all_gather(part, TCOL, axis=0, tiled=True)

    wide = exchange(copies, "mp").reshape(mp * own, rows)
    shares = exchange(partial_second(wide, total, trow), "trow")
    pieces = exchange(partial_third(shares, total, mp, at, trow), "mp")
    second = pieces[:, :, rows:].reshape(mp, own, core, share)
    second = second.transpose(1, 2, 0, 3).reshape(own, rows)
    third, numbers = coordinates(first, second, pieces, trow)
    return combined(exchange(numbers, "trow"), guess, first, second, third)


def solution(mesh):
    mp, trow, tcol = (mesh.shape[a] for a in ("mp", "trow", "tcol"))
    sizes = {"mp": mp, "trow": trow, "y": tcol // 2, "core": 2}
    split = Mesh(mesh.devices.reshape(tuple(sizes.values())), tuple(sizes))
    gram_spec = P("mp", "trow", TCOL)
    spec = P(("mp",) + TCOL, "trow")

    def body(gram, rhs, guess):
        return shards(sizes, gram, rhs, guess)

    return jax.shard_map(
        body,
        mesh=split,
        in_specs=(gram_spec, spec, spec),
        out_specs=(spec, spec),
        check_vma=False,
    )
```

```python
import jax
import jax.numpy as jnp
from jax import lax
from jax.experimental import pallas as pl
from jax.experimental.pallas import tpu as pltpu
from jax.sharding import Mesh, PartitionSpec as P

TCOL = ("y", "core")
PLANE = ("trow",) + TCOL
HIGHEST = lax.Precision.HIGHEST


def dot(lhs, rhs, lhs_dim, rhs_dim):
    return lax.dot_general(
        lhs,
        rhs,
        (((lhs_dim,), (rhs_dim,)), ((), ())),
        precision=HIGHEST,
        preferred_element_type=jnp.float32,
    )


def exchange(pieces, axes):
    return lax.all_to_all(pieces, axes, 0, 0, tiled=True)


def spread(block, axes, count):
    return exchange(jnp.broadcast_to(block[None], (count,) + block.shape), axes)


def transposed(vector, sizes):
    trow, tcol = sizes["trow"], sizes["y"] * sizes["core"]
    half = vector.shape[1] // 2
    core = lax.axis_index("core")
    halves = (vector[:, :half], vector[:, half:])
    got = []
    for turn in range(2):
        pairs = []
        for i in range(trow):
            for j in range(tcol):
                q, h = j // 2, j % 2
                pairs.append((i * tcol + j, q * tcol + 2 * i + (h ^ turn)))
        sent = jnp.where(core == turn, halves[0], halves[1])
        got.append(lax.ppermute(sent, PLANE, pairs))
    return jnp.stack(got)


def vmem_call(body, out_shape, flops, *args):
    place = pl.BlockSpec(memory_space=pltpu.VMEM)
    outs = jax.tree.leaves(out_shape)
    moved = 4 * sum(array.size for array in list(args) + outs)
    return pl.pallas_call(
        body,
        out_shape=out_shape,
        in_specs=[place] * len(args),
        out_specs=jax.tree.map(lambda _: place, out_shape),
        cost_estimate=pl.CostEstimate(flops=flops, bytes_accessed=moved, transcendentals=0),
        compiler_params=pltpu.CompilerParams(vmem_limit_bytes=16 * 2**20),
    )(*args)


def f32(*shape):
    return jax.ShapeDtypeStruct(shape, jnp.float32)


def remainder(terms, rhs):
    count = terms.shape[0]

    def body(terms_ref, rhs_ref, first_ref, out_ref):
        total = terms_ref[0]
        for n in range(1, count):
            total += terms_ref[n]
        first = rhs_ref[...] - total
        first_ref[...] = first
        for n in range(count):
            out_ref[n] = first

    return vmem_call(body, (f32(*rhs.shape), f32(*terms.shape)), 10**10, terms, rhs)


def partial_second(first, total, copies):
    count, part = first.shape[0], total.shape[0]

    def body(first_ref, total_ref, out_ref):
        second = dot(first_ref[...], total_ref[...], 1, 1)
        for n in range(copies):
            out_ref[n] = second

    out = f32(copies, count, part)
    return vmem_call(body, out, 2 * count * total.size, first, total)


def partial_third(shares, total, pieces, trow, blocks):
    count, part = shares.shape[1:]
    rows = total.shape[1]
    own, near = count // pieces, part // blocks

    def body(shares_ref, total_ref, trow_ref, out_ref):
        second = shares_ref[0]
        for n in range(1, shares.shape[0]):
            second += shares_ref[n]
        third = dot(second, total_ref[...], 1, 0)
        block = second[:, :near]
        for n in range(1, blocks):
            block = jnp.where(trow_ref[0] == n, second[:, n * near : (n + 1) * near], block)
        for n in range(pieces):
            out_ref[n, :, :rows] = third[n * own : (n + 1) * own]
            out_ref[n, :, rows:] = block[n * own : (n + 1) * own]

    place = pl.BlockSpec(memory_space=pltpu.VMEM)
    return pl.pallas_call(
        body,
        out_shape=f32(pieces, own, rows + near),
        in_specs=[place, place, pl.BlockSpec(memory_space=pltpu.SMEM)],
        out_specs=place,
        cost_estimate=pl.CostEstimate(
            flops=2 * count * total.size, bytes_accessed=4 * total.size, transcendentals=0
        ),
        compiler_params=pltpu.CompilerParams(vmem_limit_bytes=16 * 2**20),
    )(shares, total, trow)


def inner(u, v):
    return jnp.sum(u * v, axis=1, keepdims=True)


def inverse(x):
    return jnp.where(x > 0, 1.0 / jnp.where(x > 0, x, 1.0), 0.0)


def coordinates(first, second, pieces, copies):
    own, rows = first.shape

    def body(first_ref, second_ref, pieces_ref, third_ref, out_ref):
        first, second = first_ref[...], second_ref[...]
        third = pieces_ref[0, :, :rows]
        for n in range(1, pieces.shape[0]):
            third += pieces_ref[n, :, :rows]
        third_ref[...] = third
        f0 = jnp.sqrt(inner(first, first))
        e0 = first * inverse(f0)
        s0 = inner(e0, second)
        rest = second - s0 * e0
        s1 = jnp.sqrt(inner(rest, rest))
        e1 = rest * inverse(s1)
        t0 = inner(e0, third)
        t1 = inner(e1, third - t0 * e0)
        lane = lax.broadcasted_iota(jnp.int32, (own, 128), 1)
        packed = jnp.zeros((own, 128), jnp.float32)
        for n, number in enumerate((f0, s0, s1, t0, t1)):
            packed = jnp.where(lane == n, number, packed)
        for n in range(copies):
            out_ref[n] = packed

    return vmem_call(body, (f32(own, rows), f32(copies, own, 128)), pieces.size, first, second, pieces)


def combined(known, guess, first, second, third):
    blocks = known.shape[0]

    def body(known_ref, guess_ref, first_ref, second_ref, third_ref, merged_ref, residual_ref):
        parts = [known_ref[n] for n in range(blocks)]
        f0, s0, s1, t0, t1 = ([part[:, n : n + 1] for part in parts] for n in range(5))

        def total(*products):
            return sum(u * v for us, vs in products for u, v in zip(us, vs))

        norm_first = total((f0, f0))
        alpha = norm_first / total((f0, s0))
        r0 = [f - alpha * s for f, s in zip(f0, s0)]
        r1 = [-alpha * s for s in s1]
        norm_next = total((r0, r0), (r1, r1))
        beta = norm_next / norm_first
        d0 = [r + beta * f for r, f in zip(r0, f0)]
        i0 = [s - alpha * t + beta * s for s, t in zip(s0, t0)]
        i1 = [s - alpha * t + beta * s for s, t in zip(s1, t1)]
        alpha_next = norm_next / total((d0, i0), (r1, i1))

        first, second = first_ref[...], second_ref[...]
        residual = first - alpha * second
        direction = residual + beta * first
        image = second - alpha * third_ref[...] + beta * second
        merged_ref[...] = guess_ref[...] + alpha * first + alpha_next * direction
        residual_ref[...] = residual - alpha_next * image

    out = (f32(*guess.shape), f32(*guess.shape))
    return vmem_call(body, out, 16 * guess.size, known, guess, first, second, third)


def shards(sizes, gram, rhs, guess):
    mp, trow, y, core = sizes.values()
    tcol = y * core
    tile = gram[0]
    rows, cols = tile.shape
    own = rhs.shape[0]
    share = cols // mp

    part = lax.psum_scatter(tile.T, "mp", scatter_dimension=0, tiled=True)

    at, early = lax.optimization_barrier((lax.axis_index("trow").reshape(1), guess))
    over_mp = spread(transposed(early, sizes), "mp", mp)
    over_mp = over_mp.transpose(1, 0, 2, 3).reshape(2 * mp * own, cols)
    block = spread(over_mp, "trow", trow).reshape(trow, 2, mp * own, cols)
    given = dot(block[:, 1].reshape(trow * mp * own, cols), tile, 1, 1)
    given = lax.ppermute(given, "core", [(0, 1), (1, 0)])
    terms = dot(block[:, 0].reshape(trow * mp * own, cols), tile, 1, 1) + given
    terms = exchange(terms.reshape(y, mp * own, rows), "y").sum(0)
    part, _ = lax.optimization_barrier((part, terms))
    terms = exchange(terms.reshape(mp, own, rows), "mp")
    first, copies = remainder(terms, rhs)

    total = lax.all_gather(part, TCOL, axis=0, tiled=True)

    wide = exchange(copies, "mp").reshape(mp * own, rows)
    shares = exchange(partial_second(wide, total, trow), "trow")
    pieces = exchange(partial_third(shares, total, mp, at, trow), "mp")
    second = pieces[:, :, rows:].reshape(mp, own, core, share)
    second = second.transpose(1, 2, 0, 3).reshape(own, rows)
    third, numbers = coordinates(first, second, pieces, trow)
    return combined(exchange(numbers, "trow"), guess, first, second, third)


def solution(mesh):
    mp, trow, tcol = (mesh.shape[a] for a in ("mp", "trow", "tcol"))
    sizes = {"mp": mp, "trow": trow, "y": tcol // 2, "core": 2}
    split = Mesh(mesh.devices.reshape(tuple(sizes.values())), tuple(sizes))
    gram_spec = P("mp", "trow", TCOL)
    spec = P(("mp",) + TCOL, "trow")

    def body(gram, rhs, guess):
        return shards(sizes, gram, rhs, guess)

    return jax.shard_map(
        body,
        mesh=split,
        in_specs=(gram_spec, spec, spec),
        out_specs=(spec, spec),
        check_vma=False,
    )
```

```python
import jax
import jax.numpy as jnp
from jax import lax
from jax.experimental import pallas as pl
from jax.experimental.pallas import tpu as pltpu
from jax.sharding import Mesh, PartitionSpec as P

TCOL = ("y", "core")
PLANE = ("trow",) + TCOL
HIGHEST = lax.Precision.HIGHEST


def dot(lhs, rhs, lhs_dim, rhs_dim):
    return lax.dot_general(
        lhs,
        rhs,
        (((lhs_dim,), (rhs_dim,)), ((), ())),
        precision=HIGHEST,
        preferred_element_type=jnp.float32,
    )


def exchange(pieces, axes):
    return lax.all_to_all(pieces, axes, 0, 0, tiled=True)


def spread(block, axes, count):
    return exchange(jnp.broadcast_to(block[None], (count,) + block.shape), axes)


def transposed(vector, sizes):
    trow, tcol = sizes["trow"], sizes["y"] * sizes["core"]
    half = vector.shape[1] // 2
    core = lax.axis_index("core")
    halves = (vector[:, :half], vector[:, half:])
    got = []
    for turn in range(2):
        pairs = []
        for i in range(trow):
            for j in range(tcol):
                q, h = j // 2, j % 2
                pairs.append((i * tcol + j, q * tcol + 2 * i + (h ^ turn)))
        sent = jnp.where(core == turn, halves[0], halves[1])
        got.append(lax.ppermute(sent, PLANE, pairs))
    return jnp.stack(got)


def vmem_call(body, out_shape, flops, *args):
    place = pl.BlockSpec(memory_space=pltpu.VMEM)
    outs = jax.tree.leaves(out_shape)
    moved = 4 * sum(array.size for array in list(args) + outs)
    return pl.pallas_call(
        body,
        out_shape=out_shape,
        in_specs=[place] * len(args),
        out_specs=jax.tree.map(lambda _: place, out_shape),
        cost_estimate=pl.CostEstimate(flops=flops, bytes_accessed=moved, transcendentals=0),
        compiler_params=pltpu.CompilerParams(vmem_limit_bytes=16 * 2**20),
    )(*args)


def f32(*shape):
    return jax.ShapeDtypeStruct(shape, jnp.float32)


def remainder(terms, rhs):
    count = terms.shape[0]

    def body(terms_ref, rhs_ref, first_ref, out_ref):
        total = terms_ref[0]
        for n in range(1, count):
            total += terms_ref[n]
        first = rhs_ref[...] - total
        first_ref[...] = first
        for n in range(count):
            out_ref[n] = first

    return vmem_call(body, (f32(*rhs.shape), f32(*terms.shape)), terms.size, terms, rhs)


def partial_second(first, total, copies):
    count, (part, rows) = first.shape[0], total.shape
    steps = 4 if rows % 512 == 0 else 1
    chunk = rows // steps

    def body(first_ref, total_ref, out_ref, held, done):
        moves = [
            pltpu.make_async_copy(total_ref.at[:, pl.ds(n * chunk, chunk)], held.at[n], done.at[n])
            for n in range(steps)
        ]
        for move in moves:
            move.start()
        second = jnp.zeros((count, part), jnp.float32)
        for n, move in enumerate(moves):
            move.wait()
            second += dot(first_ref[:, n * chunk : (n + 1) * chunk], held[n], 1, 1)
        for n in range(copies):
            out_ref[n] = second

    place = pl.BlockSpec(memory_space=pltpu.VMEM)
    return pl.pallas_call(
        body,
        out_shape=f32(copies, count, part),
        in_specs=[place, pl.BlockSpec(memory_space=pl.ANY)],
        out_specs=place,
        scratch_shapes=[pltpu.VMEM((steps, part, chunk), jnp.float32), pltpu.SemaphoreType.DMA((steps,))],
        cost_estimate=pl.CostEstimate(
            flops=2 * count * total.size, bytes_accessed=4*total.size, transcendentals=0
        ),
        compiler_params=pltpu.CompilerParams(vmem_limit_bytes=60 * 2**20),
    )(first, total)


def partial_third(shares, total, pieces, trow, blocks):
    count, part = shares.shape[1:]
    rows = total.shape[1]
    own, near = count // pieces, part // blocks

    def body(shares_ref, total_ref, trow_ref, out_ref):
        second = shares_ref[0]
        for n in range(1, shares.shape[0]):
            second += shares_ref[n]
        third = dot(second, total_ref[...], 1, 0)
        block = second[:, :near]
        for n in range(1, blocks):
            block = jnp.where(trow_ref[0] == n, second[:, n * near : (n + 1) * near], block)
        for n in range(pieces):
            out_ref[n, :, :rows] = third[n * own : (n + 1) * own]
            out_ref[n, :, rows:] = block[n * own : (n + 1) * own]

    place = pl.BlockSpec(memory_space=pltpu.VMEM)
    return pl.pallas_call(
        body,
        out_shape=f32(pieces, own, rows + near),
        in_specs=[place, place, pl.BlockSpec(memory_space=pltpu.SMEM)],
        out_specs=place,
        cost_estimate=pl.CostEstimate(
            flops=2 * count * total.size, bytes_accessed=4 * total.size, transcendentals=0
        ),
        compiler_params=pltpu.CompilerParams(vmem_limit_bytes=16 * 2**20),
    )(shares, total, trow)


def inner(u, v):
    return jnp.sum(u * v, axis=1, keepdims=True)


def inverse(x):
    return jnp.where(x > 0, 1.0 / jnp.where(x > 0, x, 1.0), 0.0)


def coordinates(first, second, pieces, copies):
    own, rows = first.shape

    def body(first_ref, second_ref, pieces_ref, third_ref, out_ref):
        first, second = first_ref[...], second_ref[...]
        third = pieces_ref[0, :, :rows]
        for n in range(1, pieces.shape[0]):
            third += pieces_ref[n, :, :rows]
        third_ref[...] = third
        f0 = jnp.sqrt(inner(first, first))
        e0 = first * inverse(f0)
        s0 = inner(e0, second)
        rest = second - s0 * e0
        s1 = jnp.sqrt(inner(rest, rest))
        e1 = rest * inverse(s1)
        t0 = inner(e0, third)
        t1 = inner(e1, third - t0 * e0)
        lane = lax.broadcasted_iota(jnp.int32, (own, 128), 1)
        packed = jnp.zeros((own, 128), jnp.float32)
        for n, number in enumerate((f0, s0, s1, t0, t1)):
            packed = jnp.where(lane == n, number, packed)
        for n in range(copies):
            out_ref[n] = packed

    return vmem_call(body, (f32(own, rows), f32(copies, own, 128)), pieces.size, first, second, pieces)


def combined(known, guess, first, second, third):
    blocks = known.shape[0]

    def body(known_ref, guess_ref, first_ref, second_ref, third_ref, merged_ref, residual_ref):
        parts = [known_ref[n] for n in range(blocks)]
        f0, s0, s1, t0, t1 = ([part[:, n : n + 1] for part in parts] for n in range(5))

        def total(*products):
            return sum(u * v for us, vs in products for u, v in zip(us, vs))

        norm_first = total((f0, f0))
        alpha = norm_first / total((f0, s0))
        r0 = [f - alpha * s for f, s in zip(f0, s0)]
        r1 = [-alpha * s for s in s1]
        norm_next = total((r0, r0), (r1, r1))
        beta = norm_next / norm_first
        d0 = [r + beta * f for r, f in zip(r0, f0)]
        i0 = [s - alpha * t + beta * s for s, t in zip(s0, t0)]
        i1 = [s - alpha * t + beta * s for s, t in zip(s1, t1)]
        alpha_next = norm_next / total((d0, i0), (r1, i1))

        first, second = first_ref[...], second_ref[...]
        residual = first - alpha * second
        direction = residual + beta * first
        image = second - alpha * third_ref[...] + beta * second
        merged_ref[...] = guess_ref[...] + alpha * first + alpha_next * direction
        residual_ref[...] = residual - alpha_next * image

    out = (f32(*guess.shape), f32(*guess.shape))
    return vmem_call(body, out, 16 * guess.size, known, guess, first, second, third)


def shards(sizes, gram, rhs, guess):
    mp, trow, y, core = sizes.values()
    tcol = y * core
    tile = gram[0]
    rows, cols = tile.shape
    own = rhs.shape[0]
    share = cols // mp

    part = lax.psum_scatter(tile.T, "mp", scatter_dimension=0, tiled=True)

    at, early = lax.optimization_barrier((lax.axis_index("trow").reshape(1), guess))
    over_mp = spread(transposed(early, sizes), "mp", mp)
    over_mp = over_mp.transpose(1, 0, 2, 3).reshape(2 * mp * own, cols)
    block = spread(over_mp, "trow", trow).reshape(trow, 2, mp * own, cols)
    given = dot(block[:, 1].reshape(trow * mp * own, cols), tile, 1, 1)
    given = lax.ppermute(given, "core", [(0, 1), (1, 0)])
    terms = dot(block[:, 0].reshape(trow * mp * own, cols), tile, 1, 1) + given
    terms = exchange(terms.reshape(y, mp * own, rows), "y").sum(0)
    part, _ = lax.optimization_barrier((part, terms))
    terms = exchange(terms.reshape(mp, own, rows), "mp")
    first, copies = remainder(terms, rhs)

    total = lax.all_gather(part, TCOL, axis=0, tiled=True)

    wide = exchange(copies, "mp").reshape(mp * own, rows)
    shares = exchange(partial_second(wide, total, trow), "trow")
    pieces = exchange(partial_third(shares, total, mp, at, trow), "mp")
    second = pieces[:, :, rows:].reshape(mp, own, core, share)
    second = second.transpose(1, 2, 0, 3).reshape(own, rows)
    third, numbers = coordinates(first, second, pieces, trow)
    return combined(exchange(numbers, "trow"), guess, first, second, third)


def solution(mesh):
    mp, trow, tcol = (mesh.shape[a] for a in ("mp", "trow", "tcol"))
    sizes = {"mp": mp, "trow": trow, "y": tcol // 2, "core": 2}
    split = Mesh(mesh.devices.reshape(tuple(sizes.values())), tuple(sizes))
    gram_spec = P("mp", "trow", TCOL)
    spec = P(("mp",) + TCOL, "trow")

    def body(gram, rhs, guess):
        return shards(sizes, gram, rhs, guess)

    return jax.shard_map(
        body,
        mesh=split,
        in_specs=(gram_spec, spec, spec),
        out_specs=(spec, spec),
        check_vma=False,
    )
```

```python
import jax
import jax.numpy as jnp
from jax import lax
from jax.experimental import pallas as pl
from jax.experimental.pallas import tpu as pltpu
from jax.sharding import Mesh, PartitionSpec as P

TCOL = ("y", "core")
PLANE = ("trow",) + TCOL
HIGHEST = lax.Precision.HIGHEST


def dot(lhs, rhs, lhs_dim, rhs_dim):
    return lax.dot_general(
        lhs,
        rhs,
        (((lhs_dim,), (rhs_dim,)), ((), ())),
        precision=HIGHEST,
        preferred_element_type=jnp.float32,
    )


def exchange(pieces, axes):
    return lax.all_to_all(pieces, axes, 0, 0, tiled=True)


def spread(block, axes, count):
    return exchange(jnp.broadcast_to(block[None], (count,) + block.shape), axes)


def transposed(vector, sizes):
    trow, tcol = sizes["trow"], sizes["y"] * sizes["core"]
    half = vector.shape[1] // 2
    core = lax.axis_index("core")
    halves = (vector[:, :half], vector[:, half:])
    got = []
    for turn in range(2):
        pairs = []
        for i in range(trow):
            for j in range(tcol):
                q, h = j // 2, j % 2
                pairs.append((i * tcol + j, q * tcol + 2 * i + (h ^ turn)))
        sent = jnp.where(core == turn, halves[0], halves[1])
        got.append(lax.ppermute(sent, PLANE, pairs))
    return jnp.stack(got)


def vmem_call(body, out_shape, flops, *args):
    place = pl.BlockSpec(memory_space=pltpu.VMEM)
    outs = jax.tree.leaves(out_shape)
    moved = 4 * sum(array.size for array in list(args) + outs)
    return pl.pallas_call(
        body,
        out_shape=out_shape,
        in_specs=[place] * len(args),
        out_specs=jax.tree.map(lambda _: place, out_shape),
        cost_estimate=pl.CostEstimate(flops=flops, bytes_accessed=moved, transcendentals=0),
        compiler_params=pltpu.CompilerParams(vmem_limit_bytes=16 * 2**20),
    )(*args)


def f32(*shape):
    return jax.ShapeDtypeStruct(shape, jnp.float32)


def remainder(terms, rhs):
    count = terms.shape[0]

    def body(terms_ref, rhs_ref, first_ref, out_ref):
        total = terms_ref[0]
        for n in range(1, count):
            total += terms_ref[n]
        first = rhs_ref[...] - total
        first_ref[...] = first
        for n in range(count):
            out_ref[n] = first

    return vmem_call(body, (f32(*rhs.shape), f32(*terms.shape)), terms.size, terms, rhs)


def partial_second(first, total, copies):
    count, part = first.shape[0], total.shape[0]

    def body(first_ref, total_ref, out_ref):
        second = dot(first_ref[...], total_ref[...], 1, 1)
        for n in range(copies):
            out_ref[n] = second

    out = f32(copies, count, part)
    return vmem_call(body, out, 2 * count * total.size, first, total)


def partial_third(shares, total, pieces, trow, blocks):
    count, part = shares.shape[1:]
    rows = total.shape[1]
    own, near = count // pieces, part // blocks

    def body(shares_ref, total_ref, trow_ref, out_ref):
        second = shares_ref[0]
        for n in range(1, shares.shape[0]):
            second += shares_ref[n]
        third = dot(second, total_ref[...], 1, 0)
        block = second[:, :near]
        for n in range(1, blocks):
            block = jnp.where(trow_ref[0] == n, second[:, n * near : (n + 1) * near], block)
        for n in range(pieces):
            out_ref[n, :, :rows] = third[n * own : (n + 1) * own]
            out_ref[n, :, rows:] = block[n * own : (n + 1) * own]

    place = pl.BlockSpec(memory_space=pltpu.VMEM)
    return pl.pallas_call(
        body,
        out_shape=f32(pieces, own, rows + near),
        in_specs=[place, place, pl.BlockSpec(memory_space=pltpu.SMEM)],
        out_specs=place,
        cost_estimate=pl.CostEstimate(
            flops=2 * count * total.size, bytes_accessed=4 * total.size, transcendentals=0
        ),
        compiler_params=pltpu.CompilerParams(vmem_limit_bytes=16 * 2**20),
    )(shares, total, trow)


def inner(u, v):
    return jnp.sum(u * v, axis=1, keepdims=True)


def inverse(x):
    return jnp.where(x > 0, 1.0 / jnp.where(x > 0, x, 1.0), 0.0)


def coordinates(first, second, pieces, copies):
    own, rows = first.shape

    def body(first_ref, second_ref, pieces_ref, third_ref, out_ref):
        first, second = first_ref[...], second_ref[...]
        third = pieces_ref[0, :, :rows]
        for n in range(1, pieces.shape[0]):
            third += pieces_ref[n, :, :rows]
        third_ref[...] = third
        f0 = jnp.sqrt(inner(first, first))
        e0 = first * inverse(f0)
        s0 = inner(e0, second)
        rest = second - s0 * e0
        s1 = jnp.sqrt(inner(rest, rest))
        e1 = rest * inverse(s1)
        t0 = inner(e0, third)
        t1 = inner(e1, third - t0 * e0)
        lane = lax.broadcasted_iota(jnp.int32, (own, 128), 1)
        packed = jnp.zeros((own, 128), jnp.float32)
        for n, number in enumerate((f0, s0, s1, t0, t1)):
            packed = jnp.where(lane == n, number, packed)
        for n in range(copies):
            out_ref[n] = packed

    return vmem_call(body, (f32(own, rows), f32(copies, own, 128)), pieces.size, first, second, pieces)


def combined(known, guess, first, second, third):
    blocks = known.shape[0]

    def body(known_ref, guess_ref, first_ref, second_ref, third_ref, merged_ref, residual_ref):
        parts = [known_ref[n] for n in range(blocks)]
        f0, s0, s1, t0, t1 = ([part[:, n : n + 1] for part in parts] for n in range(5))

        def total(*products):
            return sum(u * v for us, vs in products for u, v in zip(us, vs))

        norm_first = total((f0, f0))
        alpha = norm_first / total((f0, s0))
        r0 = [f - alpha * s for f, s in zip(f0, s0)]
        r1 = [-alpha * s for s in s1]
        norm_next = total((r0, r0), (r1, r1))
        beta = norm_next / norm_first
        d0 = [r + beta * f for r, f in zip(r0, f0)]
        i0 = [s - alpha * t + beta * s for s, t in zip(s0, t0)]
        i1 = [s - alpha * t + beta * s for s, t in zip(s1, t1)]
        alpha_next = norm_next / total((d0, i0), (r1, i1))

        first, second = first_ref[...], second_ref[...]
        residual = first - alpha * second
        direction = residual + beta * first
        image = second - alpha * third_ref[...] + beta * second
        merged_ref[...] = guess_ref[...] + alpha * first + alpha_next * direction
        residual_ref[...] = residual - alpha_next * image

    out = (f32(*guess.shape), f32(*guess.shape))
    return vmem_call(body, out, 16 * guess.size, known, guess, first, second, third)


def shards(sizes, gram, rhs, guess):
    mp, trow, y, core = sizes.values()
    tcol = y * core
    tile = gram[0]
    rows, cols = tile.shape
    own = rhs.shape[0]
    share = cols // mp

    part = lax.psum_scatter(tile.T, "mp", scatter_dimension=0, tiled=True)

    at, early = lax.optimization_barrier((lax.axis_index("trow").reshape(1), guess))
    over_mp = spread(transposed(early, sizes), "mp", mp)
    over_mp = over_mp.transpose(1, 0, 2, 3).reshape(2 * mp * own, cols)
    block = lax.all_gather(over_mp, "trow", axis=0).reshape(trow, 2, mp * own, cols)
    given = dot(block[:, 1].reshape(trow * mp * own, cols), tile, 1, 1)
    given = lax.ppermute(given, "core", [(0, 1), (1, 0)])
    terms = dot(block[:, 0].reshape(trow * mp * own, cols), tile, 1, 1) + given
    terms = exchange(terms.reshape(y, mp * own, rows), "y").sum(0)
    part, _ = lax.optimization_barrier((part, terms))
    terms = exchange(terms.reshape(mp, own, rows), "mp")
    first, copies = remainder(terms, rhs)

    total = lax.all_gather(part, TCOL, axis=0, tiled=True)

    wide = exchange(copies, "mp").reshape(mp * own, rows)
    shares = exchange(partial_second(wide, total, trow), "trow")
    pieces = exchange(partial_third(shares, total, mp, at, trow), "mp")
    second = pieces[:, :, rows:].reshape(mp, own, core, share)
    second = second.transpose(1, 2, 0, 3).reshape(own, rows)
    third, numbers = coordinates(first, second, pieces, trow)
    return combined(exchange(numbers, "trow"), guess, first, second, third)


def solution(mesh):
    mp, trow, tcol = (mesh.shape[a] for a in ("mp", "trow", "tcol"))
    sizes = {"mp": mp, "trow": trow, "y": tcol // 2, "core": 2}
    split = Mesh(mesh.devices.reshape(tuple(sizes.values())), tuple(sizes))
    gram_spec = P("mp", "trow", TCOL)
    spec = P(("mp",) + TCOL, "trow")

    def body(gram, rhs, guess):
        return shards(sizes, gram, rhs, guess)

    return jax.shard_map(
        body,
        mesh=split,
        in_specs=(gram_spec, spec, spec),
        out_specs=(spec, spec),
        check_vma=False,
    )
```
